512 devices in a mesh: azim: 128 (over x_hi, z, y), rad: 4 (over x_lo, core).
Axes of the slice: x: 4 (x_hi: 2, x_lo: 2; x = x_hi * 2 + x_lo), y: 4, z: 16, core: 2. Of those that a mesh axis runs over, the one named last changes fastest.
Arguments:
- state: float32 [4, 5, 5, 128, 2048], P(None, None, None, 'azim', 'rad'), may hold values from -6 to 6
- rotor_trace: bfloat16 [2, 5, 5, 128, 2048], P(None, None, None, 'azim', 'rad'), may hold values from -6 to 6
- speeds: float32 [5], replicated, may hold values from 0.1 to 0.5
- mixing: float32 [5, 5], replicated, may hold values from -2.5 to 2.5
- offsets: int32 [2], replicated, may hold values from 0 to 127
- segments: int32 [2, 2048], P(None, 'rad'), may hold values from 1 to 7
Outputs:
- new_state: float32 [4, 5, 5, 128, 2048], P(None, None, None, 'azim', 'rad')
- rotor_flux: float32 [2, 5, 5, 128, 2048], P(None, None, None, 'azim', 'rad')
The draws below stay inside these ranges and needn't reach their ends.
All inputs are finite; a program needn't handle non-finite values.
Results may differ from the reference program's by a relative error of at most 0.0018.
Values may be sent and summed in bfloat16 or wider, within the bound.
A program may use at most 64 MiB of HBM per device.

```python
import math
import jax
import jax.numpy as jnp
import numpy as np
from jax import lax

V = 5
P_SIZE = 5
L = 4
STEPS = 2
SEG = 8
CA = 1
NA = 128
NK = 2048
N_AZIM = 128


def place_ends(values, stream_key, least, high):
    longest = values.shape.index(max(values.shape))
    spots = []
    for shift in (0, 1):
        where = [jax.random.randint(jax.random.fold_in(stream_key, axis), (), 0, length) for axis, length in enumerate(values.shape)]
        where[longest] = (where[longest] + shift) % values.shape[longest]
        spots.append(tuple(where))
    return values.at[spots[0]].set(least).at[spots[1]].set(high)


def shard_levels(stream_key, dims, shards, low, largest):
    factor_of, own = 1.0, jax.random.fold_in(stream_key, 6)
    for axis_at, parts in shards:
        heights = jnp.exp(jax.random.uniform(jax.random.fold_in(own, axis_at), (parts,), jnp.float32, low / len(shards), largest / len(shards)))
        factor_of = factor_of * jnp.repeat(heights, dims[axis_at] // parts).reshape([-1 if axis == axis_at else 1 for axis in range(len(dims))])
    return factor_of


def centred(own_key, shape, scale, bound, pieces=(), kind=jnp.bfloat16):
    level = shard_levels(own_key, shape, pieces, -0.22, 0.18) if pieces else 1.0
    values = jax.random.normal(own_key, shape, jnp.float32) * scale * level
    return jnp.minimum(jnp.maximum(values, -bound), bound).astype(kind)


def setup_inputs(seed: int = 0) -> dict:
    splits = jax.random.split(jax.random.key(seed), 7)
    return {
        "state": centred(splits[0], (L, V, P_SIZE, NA, NK), 1.0, 6.0, ((3, 128), (4, 4)), jnp.float32),
        "rotor_trace": centred(splits[1], (STEPS, V, P_SIZE, NA, NK), 1.0, 6.0, ((3, 128), (4, 4))),
        "speeds": jnp.clip(jnp.exp(jax.random.uniform(splits[2], (V,), jnp.float32, math.log(0.1), math.log(0.5))), 0.1, 0.5),
        "mixing": centred(splits[3], (V, V), V ** -0.5, 2.5, (), jnp.float32),
        "offsets": jax.random.randint(splits[4], (STEPS,), 0, N_AZIM).astype(jnp.int32),
        "segments": place_ends(jax.random.randint(splits[5], (STEPS, NK), 1, SEG), jax.random.fold_in(splits[5], 1), 1, SEG - 1).astype(jnp.int32),
    }


time_step = 0.05
penalty = 0.5


def basis_at(points, nodes):
    count = nodes.shape[0]
    values = np.ones((points.shape[0], count))
    for index in range(count):
        for other in range(count):
            if other != index:
                values[:, index] = values[:, index] * (points - nodes[other]) / (nodes[index] - nodes[other])
    return values


def slope_at(points, nodes):
    count = nodes.shape[0]
    values = np.zeros((points.shape[0], count))
    for index in range(count):
        for skip in range(count):
            if skip == index:
                continue
            term = np.ones(points.shape[0]) / (nodes[index] - nodes[skip])
            for other in range(count):
                if other != index and other != skip:
                    term = term * (points - nodes[other]) / (nodes[index] - nodes[other])
            values[:, index] = values[:, index] + term
    return values


def build_tables():
    nodes = (np.arange(P_SIZE) + 0.5) / P_SIZE
    deriv = slope_at(nodes, nodes)
    edge_zero = basis_at(np.array([0.0]), nodes)[0]
    edge_one = basis_at(np.array([1.0]), nodes)[0]
    table = np.zeros((SEG, P_SIZE, 2 * P_SIZE))
    for level in range(SEG):
        spots = 1.0 + nodes - level / SEG
        inside = (spots < 1.0)[:, None]
        table[level, :, :P_SIZE] = np.where(inside, basis_at(spots, nodes), 0.0)
        table[level, :, P_SIZE:] = np.where(inside, 0.0, basis_at(spots - 1.0, nodes))
    return (jnp.asarray(deriv, jnp.float32), jnp.asarray(edge_zero, jnp.float32),
            jnp.asarray(edge_one, jnp.float32), jnp.asarray(table, jnp.float32))


def mortar_values(rotated, before, seg_row, table):
    onehot = (seg_row[:, None] == jnp.arange(SEG, dtype=jnp.int32)[None, :]).astype(jnp.float32)
    per_cycle = jnp.einsum('rs,siq->iqr', onehot, table, precision=lax.Precision.HIGHEST)
    extended = jnp.concatenate([before, rotated], axis=1)
    return jnp.einsum('iqr,vqjr->vijr', per_cycle, extended, precision=lax.Precision.HIGHEST)


def edges(field, edge_zero, edge_one):
    start = jnp.einsum('k,lvkjr->lvjr', edge_zero, field, precision=lax.Precision.HIGHEST)
    finish = jnp.einsum('k,lvkjr->lvjr', edge_one, field, precision=lax.Precision.HIGHEST)
    return start, finish


def tendency(field, start, finish, left_finish, right_start, cycle_below, cycle_above, mortar, speeds, mixing, deriv):
    first = (jnp.arange(P_SIZE) == 0).astype(jnp.float32)
    final = (jnp.arange(P_SIZE) == P_SIZE - 1).astype(jnp.float32)
    local = jnp.einsum('ik,lvkjr->lvijr', deriv, field, precision=lax.Precision.HIGHEST)
    jump_left = P_SIZE * (start - left_finish)
    jump_right = penalty * P_SIZE * (right_start - finish)
    advect = local + first[None, None, :, None, None] * jump_left[:, :, None]
    result = -speeds[None, :, None, None, None] * advect + final[None, None, :, None, None] * jump_right[:, :, None]
    result = result + jnp.einsum('vw,lwijr->lvijr', mixing, field, precision=lax.Precision.HIGHEST)
    result = result + (cycle_below + cycle_above - 2.0 * field)
    below = jnp.concatenate([mortar[None], field[:-1]], axis=0)
    above = jnp.concatenate([field[1:], jnp.zeros_like(field[:1])], axis=0)
    result = result + (below + above - 2.0 * field)
    return result, mortar - field[0]


def full_tendency(field, mortar, speeds, mixing, tabs):
    deriv, edge_zero, edge_one, table = tabs
    start, finish = edges(field, edge_zero, edge_one)
    left_finish = jnp.roll(finish, 1, axis=2)
    right_start = jnp.roll(start, -1, axis=2)
    blank = jnp.zeros_like(field[..., :1])
    cycle_below = jnp.concatenate([blank, field[..., :-1]], axis=4)
    cycle_above = jnp.concatenate([field[..., 1:], blank], axis=4)
    return tendency(field, start, finish, left_finish, right_start, cycle_below, cycle_above, mortar, speeds, mixing, deriv)


def reference(state, rotor_trace, speeds, mixing, offsets, segments):
    tabs = build_tables()
    field = state
    fluxes = []
    for step in range(STEPS):
        shift = (offsets[step] * CA).astype(jnp.int32)
        rotated = jnp.roll(rotor_trace[step].astype(jnp.float32), shift, axis=2)
        before = jnp.roll(rotated, 1, axis=2)
        mortar = mortar_values(rotated, before, segments[step], tabs[3])
        rate_one, flux_one = full_tendency(field, mortar, speeds, mixing, tabs)
        middle = field + time_step * rate_one
        rate_two, flux_two = full_tendency(middle, mortar, speeds, mixing, tabs)
        field = field + 0.5 * time_step * (rate_one + rate_two)
        flux = 0.5 * (flux_one + flux_two)
        fluxes.append(jnp.roll(flux, -shift, axis=2))
    return field, jnp.stack(fluxes, axis=0)
```

```python
import functools

import jax
import jax.numpy as jnp
import numpy as np
from jax import lax
from jax.experimental import pallas as pl
from jax.experimental.pallas import tpu as pltpu
from jax.sharding import PartitionSpec as P

P_SIZE = 5
STEPS = 2
SEG = 8
V = 5
L = 4
TILE = 128
MESH = pl.DeviceIdType.MESH
time_step = 0.05
penalty = 0.5


def basis_at(points, nodes):
    count = nodes.shape[0]
    values = np.ones((points.shape[0], count))
    for index in range(count):
        for other in range(count):
            if other != index:
                values[:, index] = (
                    values[:, index] * (points - nodes[other]) / (nodes[index] - nodes[other])
                )
    return values


def slope_at(points, nodes):
    count = nodes.shape[0]
    values = np.zeros((points.shape[0], count))
    for index in range(count):
        for skip in range(count):
            if skip == index:
                continue
            term = np.ones(points.shape[0]) / (nodes[index] - nodes[skip])
            for other in range(count):
                if other != index and other != skip:
                    term = term * (points - nodes[other]) / (nodes[index] - nodes[other])
            values[:, index] = values[:, index] + term
    return values


def build_tables():
    nodes = (np.arange(P_SIZE) + 0.5) / P_SIZE
    deriv = slope_at(nodes, nodes)
    edge_zero = basis_at(np.array([0.0]), nodes)[0]
    edge_one = basis_at(np.array([1.0]), nodes)[0]
    inside = np.zeros((SEG, P_SIZE), bool)
    table = np.zeros((SEG, P_SIZE, P_SIZE))
    for level in range(SEG):
        spots = 1.0 + nodes - level / SEG
        inside[level] = spots < 1.0
        table[level] = np.where(
            inside[level][:, None], basis_at(spots, nodes), basis_at(spots - 1.0, nodes)
        )
    as_floats = lambda a: np.asarray(a, np.float32).tolist()
    return as_floats(deriv), as_floats(edge_zero), as_floats(edge_one), as_floats(table), inside


DERIV, EDGE0, EDGE1, TABLE, INSIDE = build_tables()


def iotas():
    lane = lax.broadcasted_iota(jnp.int32, (8, TILE), 1)
    row = lax.broadcasted_iota(jnp.int32, (8, TILE), 0)
    return lane, row


def weighted(weights, parts):
    total = weights[0] * parts[0]
    for weight, part in zip(weights[1:], parts[1:], strict=True):
        total = total + weight * part
    return total


def edge_values(x):
    nodes = [x[k] for k in range(P_SIZE)]
    return weighted(EDGE0, nodes), weighted(EDGE1, nodes)


def column_add(v, x, low, high):
    lane, _ = iotas()
    for i in range(P_SIZE):
        spot = v * P_SIZE + i
        low = jnp.where(lane == spot, pltpu.roll(x[i, 0], spot, 1), low)
        high = jnp.where(lane == spot, pltpu.roll(x[i, 1], spot + 1, 1), high)
    return low, high


def put_edges(v, x, starts, finishes):
    start, finish = edge_values(x)
    at = pl.ds(pl.multiple_of(v * 16, 16), 16)
    starts[at, :] = start.reshape(16, TILE)
    finishes[at, :] = finish.reshape(16, TILE)


def block_of(ref, v, rows, shape):
    return ref[pl.ds(pl.multiple_of(v * rows, rows), rows), :].reshape(shape)


def state_of(ref, v):
    return block_of(ref, v, 80, (P_SIZE, 2, 8, TILE))


def rotor_of(ref, v):
    return block_of(ref, v, 40, (P_SIZE, 8, TILE))


def rates(v, field, lefts, rights, low, high, mortar, speeds, mixing):
    lane, row = iotas()
    x = state_of(field, v)
    start, finish = edge_values(x)
    left = block_of(lefts, v, 16, (2, 8, TILE))
    right = block_of(rights, v, 16, (2, 8, TILE))
    speed = speeds[v]
    nodes = [x[k] for k in range(P_SIZE)]
    out = []
    for i in range(P_SIZE):
        slope = weighted(DERIV[i], nodes)
        if i == 0:
            slope = slope + float(P_SIZE) * (start - left)
        out.append(-speed * slope)
    out[-1] = out[-1] + (penalty * P_SIZE) * (right - finish)
    result = jnp.stack(out)
    for w in range(V):
        result = result + mixing[v, w] * state_of(field, w)
    flat = x.reshape(10, 8, TILE)
    down = pltpu.roll(flat, 1, 2).reshape(x.shape)
    up = pltpu.roll(flat, TILE - 1, 2).reshape(x.shape)
    spots = [v * P_SIZE + i for i in range(P_SIZE)]
    low_in = jnp.stack([pltpu.roll(low, lax.rem(TILE - s, TILE), 1) for s in spots])
    high_in = jnp.stack([pltpu.roll(high, TILE - 1 - s, 1) for s in spots])
    wrapped_down = jnp.where(row < 4, low_in, pltpu.roll(down[:, 1], 4, 1))
    wrapped_up = jnp.where(row >= 4, high_in, pltpu.roll(up[:, 0], 4, 1))
    below = jnp.stack(
        [
            jnp.where(lane == 0, wrapped_down, down[:, 0]),
            jnp.where(lane == 0, down[:, 0], down[:, 1]),
        ],
        axis=1,
    )
    above = jnp.stack(
        [
            jnp.where(lane == TILE - 1, up[:, 1], up[:, 0]),
            jnp.where(lane == TILE - 1, wrapped_up, up[:, 1]),
        ],
        axis=1,
    )
    layer = row % 4
    inner = pltpu.roll(flat, 1, 1).reshape(x.shape)
    outer = pltpu.roll(flat, 7, 1).reshape(x.shape)
    inner = jnp.where(layer == 0, mortar, inner)
    outer = jnp.where(layer == 3, 0.0, outer)
    return x, result + (below + above + inner + outer - 4.0 * x)


def put_packed(target, v, nodes):
    target[pl.ds(pl.multiple_of(v * 24, 24), 24), :] = pack_rows(nodes)


def mortar_tables(segment, weights, sides):
    for i in range(P_SIZE):
        side = jnp.zeros((8, TILE), jnp.float32)
        for level in range(1, SEG):
            if INSIDE[level, i]:
                side = jnp.where(segment == level, 1.0, side)
        sides[pl.ds(i * 8, 8), :] = side
        for k in range(P_SIZE):
            value = jnp.full((8, TILE), TABLE[1][i][k], jnp.float32)
            for level in range(2, SEG):
                value = jnp.where(segment == level, TABLE[level][i][k], value)
            weights[pl.ds((i * P_SIZE + k) * 8, 8), :] = value


def mortar_nodes(own, prior, weights, sides):
    out = []
    for i in range(P_SIZE):
        inside = sides[pl.ds(i * 8, 8), :] > 0.5
        picked = jnp.stack([jnp.where(inside, b, a) for a, b in zip(own, prior, strict=True)])
        factors = weights[pl.ds(i * 40, 40), :].reshape(P_SIZE, 8, TILE)
        out.append(jnp.sum(factors * picked, axis=0))
    return out


def nodes_of(ref, v):
    values = rotor_of(ref, v)
    return [values[i] for i in range(P_SIZE)]


def packed_nodes(ref, v):
    return [packed_node(ref, v, i) for i in range(P_SIZE)]


def each_variable(work):
    def one(v, carry):
        work(v)
        return carry

    lax.fori_loop(0, V, one, 0)


def sublanes(x, shift):
    return pltpu.roll(x, shift % 8, 0) if shift % 8 else x


def pack_rows(pairs):
    _, row = iotas()
    out = []
    for p in range(3):
        block = pairs[2 * p]
        if 2 * p + 1 < P_SIZE:
            block = jnp.where(row % 2 == 0, block, sublanes(pairs[2 * p + 1], 1))
        out.append(block)
    return jnp.stack(out).reshape(24, TILE)


def packed_node(ref, v, i):
    return sublanes(block_of(ref, v, 24, (3, 8, TILE))[i // 2], -(i % 2))


def stage_mortar(nodes):
    return jnp.stack([jnp.stack([x, sublanes(x, -2)]) for x in nodes])


def surface(u, mid):
    _, row = iotas()
    out = []
    for i in range(P_SIZE):
        both = 0.5 * (u[i] + mid[i])
        out.append(jnp.where(row % 4 < 2, both[0], sublanes(both[1], 2)))
    return out


class Links:
    def __init__(self, send_sem, recv_sem):
        self.send_sem, self.recv_sem, self.started = send_sem, recv_sem, []

    def send(self, source, target, device):
        at = len(self.started)
        copy = pltpu.make_async_remote_copy(
            src_ref=source,
            dst_ref=target,
            send_sem=self.send_sem.at[at],
            recv_sem=self.recv_sem.at[at],
            device_id=device,
            device_id_type=MESH,
        )
        copy.start()
        self.started.append(copy)
        return copy

    def finish(self):
        for copy in self.started:
            copy.wait_send()


def neighbours(count, width, hops):
    me, block = lax.axis_index("azim"), lax.axis_index("rad")
    along = lambda o: {"azim": lax.rem(me + o % count, count)}
    beside = lambda o: {"rad": lax.rem(block + o % width, width)}
    hops = sorted({o % count for o in hops} - {0})
    sides = sorted({1 % width, -1 % width} - {0})
    barrier = pltpu.get_barrier_semaphore()
    for o in hops:
        pl.semaphore_signal(barrier, inc=1, device_id=along(-o), device_id_type=MESH)
    for o in sides:
        pl.semaphore_signal(barrier, inc=1, device_id=beside(-o), device_id_type=MESH)
    return along, beside, lambda: pl.semaphore_wait(barrier, len(hops) + len(sides))


def send_sides(links, slot, bufs, along, beside):
    starts, finishes, lefts, rights, cols_out, cols_in = bufs
    return [
        links.send(starts.at[slot], rights.at[slot], along(-1)),
        links.send(finishes.at[slot], lefts.at[slot], along(1)),
        links.send(cols_out.at[slot, 0], cols_in.at[slot, 1], beside(-1)),
        links.send(cols_out.at[slot, 1], cols_in.at[slot, 0], beside(1)),
    ]


def columns_in(cols_in, slot, width):
    block = lax.axis_index("rad")
    low = jnp.where(block > 0, cols_in[slot, 0], 0.0)
    high = jnp.where(block < width - 1, cols_in[slot, 1], 0.0)
    return low, high


def put_columns(cols_out, slot, low, high):
    cols_out[slot, 0] = pltpu.roll(low, 4, 0)
    cols_out[slot, 1] = pltpu.roll(high, 4, 0)


def first_sides(field, slot, bufs):
    def one(v, carry):
        x = state_of(field, v)
        put_edges(v, x, bufs[0].at[slot], bufs[1].at[slot])
        return column_add(v, x, *carry)

    blank = jnp.zeros((8, TILE), jnp.float32)
    put_columns(bufs[4], slot, *lax.fori_loop(0, V, one, (blank, blank)))


def first_stage(field, mid, mortar_at, bufs, packed, speeds, mixing, width):
    low, high = columns_in(bufs[5], 0, width)

    def one(v, carry):
        x, rate = rates(
            v, field, bufs[2].at[0], bufs[3].at[0], low, high, mortar_at(v), speeds, mixing
        )
        y = x + time_step * rate
        mid[pl.ds(pl.multiple_of(v * 80, 80), 80), :] = y.reshape(80, TILE)
        put_edges(v, y, bufs[0].at[1], bufs[1].at[1])
        put_packed(packed, v, surface(x, y))
        return column_add(v, y, *carry)

    blank = jnp.zeros((8, TILE), jnp.float32)
    put_columns(bufs[4], 1, *lax.fori_loop(0, V, one, (blank, blank)))


def second_stage(field, mid, mortar_at, bufs, target, speeds, mixing, width):
    low, high = columns_in(bufs[5], 1, width)

    def one(v, carry):
        y, rate = rates(
            v, mid, bufs[2].at[1], bufs[3].at[1], low, high, mortar_at(v), speeds, mixing
        )
        new = 0.5 * (state_of(field, v) + y) + (0.5 * time_step) * rate
        target[pl.ds(pl.multiple_of(v * 80, 80), 80), :] = new.reshape(80, TILE)
        return carry

    lax.fori_loop(0, V, one, 0)


def near_step(step, count, width, *refs):
    (
        field, rotor, segment, speeds, mixing, field_out, flux_out,
        mid, own, seen, weights, sides, halves, seam, unpacked,
        starts, finishes, lefts, rights, cols_out, cols_in, send_sem, recv_sem,
    ) = refs
    along, beside, entered = neighbours(count, width, (1, -1))
    bufs = (starts, finishes, lefts, rights, cols_out, cols_in)
    own[...] = rotor[...].astype(jnp.float32)
    unpacked[...] = jnp.zeros_like(unpacked)
    each_variable(
        lambda v: put_packed(unpacked, v, [sublanes(x, -step) for x in nodes_of(own, v)])
    )
    halves[...] = unpacked[...].astype(jnp.bfloat16)
    first_sides(field, 0, bufs)
    mortar_tables(segment[...], weights, sides)

    entered()
    links = Links(send_sem, recv_sem)
    near = send_sides(links, 0, bufs, along, beside)
    near.append(links.send(halves, seam, along(1)))
    for copy in near:
        copy.wait_recv()
    unpacked[...] = seam[...].astype(jnp.float32)

    def faced(v):
        before = [sublanes(x, step) for x in packed_nodes(unpacked, v)]
        values = mortar_nodes(nodes_of(own, v), before, weights, sides)
        put_packed(seen, v, [sublanes(x, -step) for x in values])

    each_variable(faced)
    mortar_at = lambda v: stage_mortar(packed_nodes(seen, v))
    first_stage(field, mid, mortar_at, bufs, flux_out, speeds, mixing, width)
    near = send_sides(links, 1, bufs, along, beside)
    flux_out[...] = seen[...] - flux_out[...]
    for copy in near:
        copy.wait_recv()
    second_stage(field, mid, mortar_at, bufs, field_out, speeds, mixing, width)
    links.finish()


VMEM = pl.BlockSpec(memory_space=pltpu.VMEM)
SMEM = pl.BlockSpec(memory_space=pltpu.SMEM)


def rows(*shape):
    return pltpu.VMEM((*shape, TILE), jnp.float32)


def side_buffers():
    return [rows(2, 80) for _ in range(4)] + [rows(2, 2, 8), rows(2, 2, 8)]


def links_buffers():
    return [pltpu.SemaphoreType.DMA((9,)), pltpu.SemaphoreType.DMA((9,))]


def shaped(*shape):
    return jax.ShapeDtypeStruct(shape, jnp.float32)


def call_step(step, count, width, field, rotor, segment, speeds, mixing):
    half = pltpu.VMEM((TILE, TILE), jnp.bfloat16)
    return pl.pallas_call(
        functools.partial(near_step, step, count, width),
        out_shape=(shaped(400, TILE), shaped(120, TILE)),
        in_specs=[VMEM, VMEM, VMEM, SMEM, SMEM],
        out_specs=(VMEM, VMEM),
        scratch_shapes=[rows(400), rows(200), rows(120), rows(200), rows(40), half, half]
        + [rows(TILE)]
        + side_buffers()
        + links_buffers(),
        compiler_params=pltpu.CompilerParams(
            collective_id=step, has_side_effects=True, vmem_limit_bytes=16 << 20
        ),
    )(field, rotor, segment, speeds, mixing)


def passed_along(block, distance):
    count = lax.axis_size("azim")
    return lax.ppermute(block, "azim", [(i, (i + distance) % count) for i in range(count)])


def shifted(block, offset, sign):
    moves = [functools.partial(passed_along, distance=sign * d) for d in range(lax.axis_size("azim"))]
    return lax.switch(offset, moves, block)


def unpacked_flux(packed):
    nodes = packed.reshape(V, 3, 4, 2, TILE).transpose(0, 1, 3, 2, 4)
    return nodes.reshape(V, 6, 1, 4 * TILE)[:, :P_SIZE]


def body(count, width, state, rotor_trace, speeds, mixing, offsets, segments):
    field = state.reshape(L, V, P_SIZE, 2, 2, TILE).transpose(1, 2, 4, 3, 0, 5)
    rotor = rotor_trace.reshape(STEPS, V, P_SIZE, 4, TILE).transpose(1, 2, 3, 0, 4)
    segment = segments.reshape(STEPS, 4, TILE).transpose(1, 0, 2)
    field, rotor, segment = (x.reshape(-1, TILE) for x in (field, rotor, segment))
    fluxes = []
    for step in range(STEPS):
        faced = shifted(rotor, offsets[step], 1)
        field, flux = call_step(step, count, width, field, faced, segment, speeds, mixing)
        fluxes.append(shifted(flux, offsets[step], -1))
    new_state = field.reshape(V, P_SIZE, 2, 2, L, TILE).transpose(4, 0, 1, 3, 2, 5)
    rotor_flux = jnp.stack([unpacked_flux(flux) for flux in fluxes])
    return new_state.reshape(state.shape), rotor_flux


def solution(mesh):
    cells = P(None, None, None, "azim", "rad")
    return jax.shard_map(
        functools.partial(body, mesh.shape["azim"], mesh.shape["rad"]),
        mesh=mesh,
        in_specs=(cells, cells, P(), P(), P(), P(None, "rad")),
        out_specs=(cells, cells),
        check_vma=False,
    )
```

```python
import functools

import jax
import jax.numpy as jnp
import numpy as np
from jax import lax
from jax.experimental import pallas as pl
from jax.experimental.pallas import tpu as pltpu
from jax.sharding import PartitionSpec as P

P_SIZE = 5
STEPS = 2
SEG = 8
UNROLL = True
V = 5
L = 4
TILE = 128
MESH = pl.DeviceIdType.MESH
time_step = 0.05
penalty = 0.5


def basis_at(points, nodes):
    count = nodes.shape[0]
    values = np.ones((points.shape[0], count))
    for index in range(count):
        for other in range(count):
            if other != index:
                values[:, index] = (
                    values[:, index] * (points - nodes[other]) / (nodes[index] - nodes[other])
                )
    return values


def slope_at(points, nodes):
    count = nodes.shape[0]
    values = np.zeros((points.shape[0], count))
    for index in range(count):
        for skip in range(count):
            if skip == index:
                continue
            term = np.ones(points.shape[0]) / (nodes[index] - nodes[skip])
            for other in range(count):
                if other != index and other != skip:
                    term = term * (points - nodes[other]) / (nodes[index] - nodes[other])
            values[:, index] = values[:, index] + term
    return values


def build_tables():
    nodes = (np.arange(P_SIZE) + 0.5) / P_SIZE
    deriv = slope_at(nodes, nodes)
    edge_zero = basis_at(np.array([0.0]), nodes)[0]
    edge_one = basis_at(np.array([1.0]), nodes)[0]
    inside = np.zeros((SEG, P_SIZE), bool)
    table = np.zeros((SEG, P_SIZE, P_SIZE))
    for level in range(SEG):
        spots = 1.0 + nodes - level / SEG
        inside[level] = spots < 1.0
        table[level] = np.where(
            inside[level][:, None], basis_at(spots, nodes), basis_at(spots - 1.0, nodes)
        )
    as_floats = lambda a: np.asarray(a, np.float32).tolist()
    return as_floats(deriv), as_floats(edge_zero), as_floats(edge_one), as_floats(table), inside


DERIV, EDGE0, EDGE1, TABLE, INSIDE = build_tables()


def iotas():
    lane = lax.broadcasted_iota(jnp.int32, (8, TILE), 1)
    row = lax.broadcasted_iota(jnp.int32, (8, TILE), 0)
    return lane, row


def weighted(weights, parts):
    total = weights[0] * parts[0]
    for weight, part in zip(weights[1:], parts[1:], strict=True):
        total = total + weight * part
    return total


def edge_values(x):
    nodes = [x[k] for k in range(P_SIZE)]
    return weighted(EDGE0, nodes), weighted(EDGE1, nodes)


def column_add(v, x, low, high):
    lane, _ = iotas()
    for i in range(P_SIZE):
        spot = v * P_SIZE + i
        low = jnp.where(lane == spot, pltpu.roll(x[i, 0], spot, 1), low)
        high = jnp.where(lane == spot, pltpu.roll(x[i, 1], spot + 1, 1), high)
    return low, high


def put_edges(v, x, starts, finishes):
    start, finish = edge_values(x)
    at = pl.ds(pl.multiple_of(v * 16, 16), 16)
    starts[at, :] = start.reshape(16, TILE)
    finishes[at, :] = finish.reshape(16, TILE)


def block_of(ref, v, rows, shape):
    return ref[pl.ds(pl.multiple_of(v * rows, rows), rows), :].reshape(shape)


def state_of(ref, v):
    return block_of(ref, v, 80, (P_SIZE, 2, 8, TILE))


def rotor_of(ref, v):
    return block_of(ref, v, 40, (P_SIZE, 8, TILE))


def rates(v, field, lefts, rights, low, high, speeds, mixing):
    lane, row = iotas()
    x = state_of(field, v)
    start, finish = edge_values(x)
    left = block_of(lefts, v, 16, (2, 8, TILE))
    right = block_of(rights, v, 16, (2, 8, TILE))
    speed = speeds[v]
    nodes = [x[k] for k in range(P_SIZE)]
    out = []
    for i in range(P_SIZE):
        slope = weighted(DERIV[i], nodes)
        if i == 0:
            slope = slope + float(P_SIZE) * (start - left)
        out.append(-speed * slope)
    out[-1] = out[-1] + (penalty * P_SIZE) * (right - finish)
    result = jnp.stack(out)
    for w in range(V):
        result = result + mixing[v, w] * state_of(field, w)
    flat = x.reshape(10, 8, TILE)
    down = pltpu.roll(flat, 1, 2).reshape(x.shape)
    up = pltpu.roll(flat, TILE - 1, 2).reshape(x.shape)
    spots = [v * P_SIZE + i for i in range(P_SIZE)]
    low_in = jnp.stack([pltpu.roll(low, lax.rem(TILE - s, TILE), 1) for s in spots])
    high_in = jnp.stack([pltpu.roll(high, TILE - 1 - s, 1) for s in spots])
    wrapped_down = jnp.where(row < 4, low_in, pltpu.roll(down[:, 1], 4, 1))
    wrapped_up = jnp.where(row >= 4, high_in, pltpu.roll(up[:, 0], 4, 1))
    below = jnp.stack(
        [
            jnp.where(lane == 0, wrapped_down, down[:, 0]),
            jnp.where(lane == 0, down[:, 0], down[:, 1]),
        ],
        axis=1,
    )
    above = jnp.stack(
        [
            jnp.where(lane == TILE - 1, up[:, 1], up[:, 0]),
            jnp.where(lane == TILE - 1, wrapped_up, up[:, 1]),
        ],
        axis=1,
    )
    layer = row % 4
    inner = pltpu.roll(flat, 1, 1).reshape(x.shape)
    outer = pltpu.roll(flat, 7, 1).reshape(x.shape)
    inner = jnp.where(layer == 0, 0.0, inner)
    outer = jnp.where(layer == 3, 0.0, outer)
    return x, result + (below + above + inner + outer - 4.0 * x)


def put_packed(target, v, nodes):
    target[pl.ds(pl.multiple_of(v * 24, 24), 24), :] = pack_rows(nodes)


def mortar_tables(segment, weights, sides):
    for i in range(P_SIZE):
        side = jnp.zeros((8, TILE), jnp.float32)
        for level in range(1, SEG):
            if INSIDE[level, i]:
                side = jnp.where(segment == level, 1.0, side)
        sides[pl.ds(i * 8, 8), :] = side
        for k in range(P_SIZE):
            value = jnp.full((8, TILE), TABLE[1][i][k], jnp.float32)
            for level in range(2, SEG):
                value = jnp.where(segment == level, TABLE[level][i][k], value)
            weights[pl.ds((i * P_SIZE + k) * 8, 8), :] = value


def mortar_nodes(own, prior, weights, sides):
    out = []
    for i in range(P_SIZE):
        inside = sides[pl.ds(i * 8, 8), :] > 0.5
        picked = jnp.stack([jnp.where(inside, b, a) for a, b in zip(own, prior, strict=True)])
        factors = weights[pl.ds(i * 40, 40), :].reshape(P_SIZE, 8, TILE)
        out.append(jnp.sum(factors * picked, axis=0))
    return out


def nodes_of(ref, v):
    values = rotor_of(ref, v)
    return [values[i] for i in range(P_SIZE)]


def packed_nodes(ref, v):
    return [packed_node(ref, v, i) for i in range(P_SIZE)]


def each_variable(work):
    def one(v, carry):
        work(v)
        return carry

    lax.fori_loop(0, V, one, 0, unroll=UNROLL)


def sublanes(x, shift):
    return pltpu.roll(x, shift % 8, 0) if shift % 8 else x


def pack_rows(pairs):
    _, row = iotas()
    out = []
    for p in range(3):
        block = pairs[2 * p]
        if 2 * p + 1 < P_SIZE:
            block = jnp.where(row % 2 == 0, block, sublanes(pairs[2 * p + 1], 1))
        out.append(block)
    return jnp.stack(out).reshape(24, TILE)


def packed_node(ref, v, i):
    return sublanes(block_of(ref, v, 24, (3, 8, TILE))[i // 2], -(i % 2))


def stage_mortar(nodes):
    _, row = iotas()
    spread = jnp.stack([jnp.stack([x, sublanes(x, -2)]) for x in nodes])
    return jnp.where(row % 4 == 0, spread, 0.0)


def surface(x, rate):
    _, row = iotas()
    out = []
    for i in range(P_SIZE):
        both = x[i] + (0.5 * time_step) * rate[i]
        out.append(jnp.where(row % 4 < 2, both[0], sublanes(both[1], 2)))
    return out


class Links:
    def __init__(self, send_sem, recv_sem):
        self.send_sem, self.recv_sem, self.started = send_sem, recv_sem, []

    def send(self, source, target, device):
        at = len(self.started)
        copy = pltpu.make_async_remote_copy(
            src_ref=source,
            dst_ref=target,
            send_sem=self.send_sem.at[at],
            recv_sem=self.recv_sem.at[at],
            device_id=device,
            device_id_type=MESH,
        )
        copy.start()
        self.started.append(copy)
        return copy

    def finish(self):
        for copy in self.started:
            copy.wait_send()


def neighbours(count, width, hops):
    me, block = lax.axis_index("azim"), lax.axis_index("rad")
    along = lambda o: {"azim": lax.rem(me + o % count, count)}
    beside = lambda o: {"rad": lax.rem(block + o % width, width)}
    hops = sorted({o % count for o in hops} - {0})
    sides = sorted({1 % width, -1 % width} - {0})
    barrier = pltpu.get_barrier_semaphore()
    for o in hops:
        pl.semaphore_signal(barrier, inc=1, device_id=along(-o), device_id_type=MESH)
    for o in sides:
        pl.semaphore_signal(barrier, inc=1, device_id=beside(-o), device_id_type=MESH)
    return along, beside, lambda: pl.semaphore_wait(barrier, len(hops) + len(sides))


def send_sides(links, slot, bufs, along, beside):
    starts, finishes, lefts, rights, cols_out, cols_in = bufs
    return [
        links.send(starts.at[slot], rights.at[slot], along(-1)),
        links.send(finishes.at[slot], lefts.at[slot], along(1)),
        links.send(cols_out.at[slot, 0], cols_in.at[slot, 1], beside(-1)),
        links.send(cols_out.at[slot, 1], cols_in.at[slot, 0], beside(1)),
    ]


def columns_in(cols_in, slot, width):
    block = lax.axis_index("rad")
    low = jnp.where(block > 0, cols_in[slot, 0], 0.0)
    high = jnp.where(block < width - 1, cols_in[slot, 1], 0.0)
    return low, high


def put_columns(cols_out, slot, low, high):
    cols_out[slot, 0] = pltpu.roll(low, 4, 0)
    cols_out[slot, 1] = pltpu.roll(high, 4, 0)


def each_with_sides(work, slot, bufs):
    def one(v, carry):
        x = work(v)
        put_edges(v, x, bufs[0].at[slot], bufs[1].at[slot])
        return column_add(v, x, *carry)

    blank = jnp.zeros((8, TILE), jnp.float32)
    low, high = lax.fori_loop(0, V, one, (blank, blank), unroll=UNROLL)
    put_columns(bufs[4], slot, low, high)


def put_state(target, v, x):
    target[pl.ds(pl.multiple_of(v * 80, 80), 80), :] = x.reshape(80, TILE)


def begin(field, rate, mortar, mid, slot, bufs):
    def work(v):
        full = state_of(rate, v) + stage_mortar(packed_nodes(mortar, v))
        y = state_of(field, v) + time_step * full
        put_state(mid, v, y)
        return y

    each_with_sides(work, slot, bufs)


def conclude(field, mid, mortar, slot, bufs, speeds, mixing, width, target):
    low, high = columns_in(bufs[5], slot, width)

    def work(v):
        y, rate = rates(v, mid, bufs[2].at[slot], bufs[3].at[slot], low, high, speeds, mixing)
        full = rate + stage_mortar(packed_nodes(mortar, v))
        new = 0.5 * (state_of(field, v) + y) + (0.5 * time_step) * full
        put_state(target, v, new)
        return new

    return work


def look_ahead(field, slot, bufs, speeds, mixing, width, rate_out, back_out):
    low, high = columns_in(bufs[5], slot, width)

    def work(v):
        x, rate = rates(v, field, bufs[2].at[slot], bufs[3].at[slot], low, high, speeds, mixing)
        put_state(rate_out, v, rate)
        put_packed(back_out, v, surface(x, rate))

    each_variable(work)


def opening(count, width, *refs):
    (
        field, rotor, segment, speeds, mixing, rate_out, back_out, ready_out,
        own, weights, sides, wide, halves, seam, *rest,
    ) = refs
    *bufs, send_sem, recv_sem = rest
    along, beside, entered = neighbours(count, width, (1, -1))
    own[...] = rotor[...].astype(jnp.float32)
    wide[...] = jnp.zeros_like(wide)
    for step in range(STEPS):
        each_variable(
            lambda v, step=step: put_packed(
                wide.at[step], v, [sublanes(x, -step) for x in nodes_of(own, v)]
            )
        )
    halves[...] = wide[...].astype(jnp.bfloat16)
    each_with_sides(lambda v: state_of(field, v), 0, bufs)

    entered()
    links = Links(send_sem, recv_sem)
    near = send_sides(links, 0, bufs, along, beside)
    seam_copy = links.send(halves, seam, along(1))
    mortar_tables(segment[...], weights, sides)
    for copy in near:
        copy.wait_recv()
    look_ahead(field, 0, bufs, speeds, mixing, width, rate_out, back_out)
    seam_copy.wait_recv()
    wide[...] = seam[...].astype(jnp.float32)
    for step in range(STEPS):

        def facing(v, step=step):
            before = [sublanes(x, step) for x in packed_nodes(wide.at[step], v)]
            values = mortar_nodes(nodes_of(own, v), before, weights, sides)
            put_packed(ready_out.at[step], v, [sublanes(x, -step) for x in values])

        each_variable(facing)
    links.finish()


def first_step(count, width, *refs):
    field, rate, mortar, speeds, mixing, field_out, rate_out, back_out, mid, *rest = refs
    *bufs, send_sem, recv_sem = rest
    along, beside, entered = neighbours(count, width, (1, -1))
    begin(field, rate, mortar, mid, 0, bufs)
    entered()
    links = Links(send_sem, recv_sem)
    for copy in send_sides(links, 0, bufs, along, beside):
        copy.wait_recv()
    work = conclude(field, mid, mortar, 0, bufs, speeds, mixing, width, field_out)
    each_with_sides(work, 1, bufs)
    for copy in send_sides(links, 1, bufs, along, beside):
        copy.wait_recv()
    look_ahead(field_out, 1, bufs, speeds, mixing, width, rate_out, back_out)
    links.finish()


def last_step(count, width, *refs):
    (
        field, rate, mortar, ready, first_back, second_back, speeds, mixing,
        field_out, flux_out, mid, *rest,
    ) = refs
    *bufs, send_sem, recv_sem = rest
    along, beside, entered = neighbours(count, width, (1, -1))
    begin(field, rate, mortar, mid, 0, bufs)
    entered()
    links = Links(send_sem, recv_sem)
    near = send_sides(links, 0, bufs, along, beside)
    _, row = iotas()

    def flux(v):
        both = []
        for step, back in enumerate((first_back, second_back)):
            own, seen = packed_nodes(ready.at[step], v), packed_nodes(back, v)
            both.append([(1.0 - 0.5 * time_step) * a - b for a, b in zip(own, seen, strict=True)])
        nodes = [jnp.where(row % 2 == 0, a, sublanes(b, 1)) for a, b in zip(*both, strict=True)]
        flux_out[pl.ds(pl.multiple_of(v * 40, 40), 40), :] = jnp.stack(nodes).reshape(40, TILE)

    each_variable(flux)
    for copy in near:
        copy.wait_recv()
    each_variable(conclude(field, mid, mortar, 0, bufs, speeds, mixing, width, field_out))
    links.finish()


def swap(shift, count, ready, back, mortar_out, back_out, send_sem, recv_sem):
    me = lax.axis_index("azim")
    links = Links(send_sem, recv_sem)
    there, here = ({"azim": lax.rem(me + o % count, count)} for o in (shift, -shift))
    copies = [links.send(ready, mortar_out, there), links.send(back, back_out, here)]
    for copy in copies:
        copy.wait_recv()
    links.finish()


VMEM = pl.BlockSpec(memory_space=pltpu.VMEM)
ANY = pl.BlockSpec(memory_space=pl.ANY)
SMEM = pl.BlockSpec(memory_space=pltpu.SMEM)


def rows(*shape):
    return pltpu.VMEM((*shape, TILE), jnp.float32)


def side_buffers():
    return [rows(2, 80) for _ in range(4)] + [rows(2, 2, 8), rows(2, 2, 8)]


def links_buffers(copies):
    return [pltpu.SemaphoreType.DMA((copies,)), pltpu.SemaphoreType.DMA((copies,))]


def shaped(*shape):
    return jax.ShapeDtypeStruct(shape, jnp.float32)


def call(kernel, identity, outs, scratch, copies, *operands):
    slots = len(operands) - 2
    return pl.pallas_call(
        kernel,
        out_shape=tuple(shaped(*out, TILE) for out in outs),
        in_specs=[VMEM] * slots + [SMEM, SMEM],
        out_specs=(VMEM,) * len(outs),
        scratch_shapes=scratch + side_buffers() + links_buffers(copies),
        compiler_params=pltpu.CompilerParams(
            collective_id=identity, has_side_effects=True, vmem_limit_bytes=16 << 20
        ),
    )(*operands)


def call_swap(shift, count, ready, back):
    if shift % count == 0:
        return ready, back
    return pl.pallas_call(
        functools.partial(swap, shift, count),
        out_shape=(shaped(*ready.shape), shaped(*back.shape)),
        in_specs=[ANY, ANY],
        out_specs=(ANY, ANY),
        scratch_shapes=links_buffers(2),
        compiler_params=pltpu.CompilerParams(has_side_effects=True),
    )(ready, back)


def body(count, width, state, rotor_trace, speeds, mixing, offsets, segments):
    field = state.reshape(L, V, P_SIZE, 2, 2, TILE).transpose(1, 2, 4, 3, 0, 5)
    rotor = rotor_trace.reshape(STEPS, V, P_SIZE, 4, TILE).transpose(1, 2, 3, 0, 4)
    segment = segments.reshape(STEPS, 4, TILE).transpose(1, 0, 2)
    field, rotor, segment = (x.reshape(-1, TILE) for x in (field, rotor, segment))
    swaps = [functools.partial(call_swap, shift, count) for shift in range(count)]
    bind = lambda kernel: functools.partial(kernel, count, width)
    half = pltpu.VMEM((STEPS, TILE, TILE), jnp.bfloat16)

    rate, back, ready = call(
        bind(opening), 0, ((400,), (120,), (STEPS, 120)),
        [rows(200), rows(200), rows(40), rows(STEPS, TILE), half, half], 5,
        field, rotor, segment, speeds, mixing,
    )
    mortar, first_back = lax.switch(offsets[0], swaps, ready[0], back)
    field, rate, back = call(
        bind(first_step), 1, ((400,), (400,), (120,)), [rows(400)], 8,
        field, rate, mortar, speeds, mixing,
    )
    mortar, second_back = lax.switch(offsets[1], swaps, ready[1], back)
    field, flux = call(
        bind(last_step), 2, ((400,), (200,)), [rows(400)], 4,
        field, rate, mortar, ready, first_back, second_back, speeds, mixing,
    )
    new_state = field.reshape(V, P_SIZE, 2, 2, L, TILE).transpose(4, 0, 1, 3, 2, 5)
    rotor_flux = flux.reshape(V, P_SIZE, 4, STEPS, TILE).transpose(3, 0, 1, 2, 4)
    return new_state.reshape(state.shape), rotor_flux.reshape(rotor_trace.shape)


def solution(mesh):
    cells = P(None, None, None, "azim", "rad")
    return jax.shard_map(
        functools.partial(body, mesh.shape["azim"], mesh.shape["rad"]),
        mesh=mesh,
        in_specs=(cells, cells, P(), P(), P(), P(None, "rad")),
        out_specs=(cells, cells),
        check_vma=False,
    )
```

```python
import functools

import jax
import jax.numpy as jnp
import numpy as np
from jax import lax
from jax.experimental import pallas as pl
from jax.experimental.pallas import tpu as pltpu
from jax.sharding import PartitionSpec as P

P_SIZE = 5
STEPS = 2
SEG = 8
UNROLL = True
V = 5
L = 4
TILE = 128
MESH = pl.DeviceIdType.MESH
time_step = 0.05
penalty = 0.5


def basis_at(points, nodes):
    count = nodes.shape[0]
    values = np.ones((points.shape[0], count))
    for index in range(count):
        for other in range(count):
            if other != index:
                values[:, index] = (
                    values[:, index] * (points - nodes[other]) / (nodes[index] - nodes[other])
                )
    return values


def slope_at(points, nodes):
    count = nodes.shape[0]
    values = np.zeros((points.shape[0], count))
    for index in range(count):
        for skip in range(count):
            if skip == index:
                continue
            term = np.ones(points.shape[0]) / (nodes[index] - nodes[skip])
            for other in range(count):
                if other != index and other != skip:
                    term = term * (points - nodes[other]) / (nodes[index] - nodes[other])
            values[:, index] = values[:, index] + term
    return values


def build_tables():
    nodes = (np.arange(P_SIZE) + 0.5) / P_SIZE
    deriv = slope_at(nodes, nodes)
    edge_zero = basis_at(np.array([0.0]), nodes)[0]
    edge_one = basis_at(np.array([1.0]), nodes)[0]
    inside = np.zeros((SEG, P_SIZE), bool)
    table = np.zeros((SEG, P_SIZE, P_SIZE))
    for level in range(SEG):
        spots = 1.0 + nodes - level / SEG
        inside[level] = spots < 1.0
        table[level] = np.where(
            inside[level][:, None], basis_at(spots, nodes), basis_at(spots - 1.0, nodes)
        )
    as_floats = lambda a: np.asarray(a, np.float32).tolist()
    return as_floats(deriv), as_floats(edge_zero), as_floats(edge_one), as_floats(table), inside


DERIV, EDGE0, EDGE1, TABLE, INSIDE = build_tables()


def iotas():
    lane = lax.broadcasted_iota(jnp.int32, (8, TILE), 1)
    row = lax.broadcasted_iota(jnp.int32, (8, TILE), 0)
    return lane, row


def weighted(weights, parts):
    total = weights[0] * parts[0]
    for weight, part in zip(weights[1:], parts[1:], strict=True):
        total = total + weight * part
    return total


def edge_values(x):
    nodes = [x[k] for k in range(P_SIZE)]
    return weighted(EDGE0, nodes), weighted(EDGE1, nodes)


def column_add(v, x, low, high):
    lane, _ = iotas()
    for i in range(P_SIZE):
        spot = v * P_SIZE + i
        low = jnp.where(lane == spot, pltpu.roll(x[i, 0], spot, 1), low)
        high = jnp.where(lane == spot, pltpu.roll(x[i, 1], spot + 1, 1), high)
    return low, high


def put_edges(v, x, starts, finishes):
    start, finish = edge_values(x)
    at = pl.ds(pl.multiple_of(v * 16, 16), 16)
    starts[at, :] = start.reshape(16, TILE)
    finishes[at, :] = finish.reshape(16, TILE)


def block_of(ref, v, rows, shape):
    return ref[pl.ds(pl.multiple_of(v * rows, rows), rows), :].reshape(shape)


def state_of(ref, v):
    return block_of(ref, v, 80, (P_SIZE, 2, 8, TILE))


def rotor_of(ref, v):
    return block_of(ref, v, 40, (P_SIZE, 8, TILE))


def rates(v, field, lefts, rights, low, high, speeds, mixing):
    lane, row = iotas()
    x = state_of(field, v)
    start, finish = edge_values(x)
    jump_left, jump_right = start, -finish
    if lefts is not None:
        jump_left = start - block_of(lefts, v, 16, (2, 8, TILE))
        jump_right = block_of(rights, v, 16, (2, 8, TILE)) - finish
    speed = speeds[v]
    nodes = [x[k] for k in range(P_SIZE)]
    out = []
    for i in range(P_SIZE):
        slope = weighted(DERIV[i], nodes)
        if i == 0:
            slope = slope + float(P_SIZE) * jump_left
        out.append(-speed * slope)
    out[-1] = out[-1] + (penalty * P_SIZE) * jump_right
    result = jnp.stack(out)
    for w in range(V):
        result = result + mixing[v, w] * state_of(field, w)
    flat = x.reshape(10, 8, TILE)
    down = pltpu.roll(flat, 1, 2).reshape(x.shape)
    up = pltpu.roll(flat, TILE - 1, 2).reshape(x.shape)
    spots = [v * P_SIZE + i for i in range(P_SIZE)]
    if low is None:
        low_in = high_in = 0.0
    else:
        low_in = jnp.stack([pltpu.roll(low, lax.rem(TILE - s, TILE), 1) for s in spots])
        high_in = jnp.stack([pltpu.roll(high, TILE - 1 - s, 1) for s in spots])
    wrapped_down = jnp.where(row < 4, low_in, pltpu.roll(down[:, 1], 4, 1))
    wrapped_up = jnp.where(row >= 4, high_in, pltpu.roll(up[:, 0], 4, 1))
    below = jnp.stack(
        [
            jnp.where(lane == 0, wrapped_down, down[:, 0]),
            jnp.where(lane == 0, down[:, 0], down[:, 1]),
        ],
        axis=1,
    )
    above = jnp.stack(
        [
            jnp.where(lane == TILE - 1, up[:, 1], up[:, 0]),
            jnp.where(lane == TILE - 1, wrapped_up, up[:, 1]),
        ],
        axis=1,
    )
    layer = row % 4
    inner = pltpu.roll(flat, 1, 1).reshape(x.shape)
    outer = pltpu.roll(flat, 7, 1).reshape(x.shape)
    inner = jnp.where(layer == 0, 0.0, inner)
    outer = jnp.where(layer == 3, 0.0, outer)
    return x, result + (below + above + inner + outer - 4.0 * x)


def put_packed(target, v, nodes):
    target[pl.ds(pl.multiple_of(v * 24, 24), 24), :] = pack_rows(nodes)


def mortar_tables(segment, weights, sides):
    for i in range(P_SIZE):
        side = jnp.zeros((8, TILE), jnp.float32)
        for level in range(1, SEG):
            if INSIDE[level, i]:
                side = jnp.where(segment == level, 1.0, side)
        sides[pl.ds(i * 8, 8), :] = side
        for k in range(P_SIZE):
            value = jnp.full((8, TILE), TABLE[1][i][k], jnp.float32)
            for level in range(2, SEG):
                value = jnp.where(segment == level, TABLE[level][i][k], value)
            weights[pl.ds((i * P_SIZE + k) * 8, 8), :] = value


def mortar_nodes(own, prior, weights, sides):
    out = []
    for i in range(P_SIZE):
        inside = sides[pl.ds(i * 8, 8), :] > 0.5
        picked = jnp.stack([jnp.where(inside, b, a) for a, b in zip(own, prior, strict=True)])
        factors = weights[pl.ds(i * 40, 40), :].reshape(P_SIZE, 8, TILE)
        out.append(jnp.sum(factors * picked, axis=0))
    return out


def nodes_of(ref, v):
    values = rotor_of(ref, v)
    return [values[i] for i in range(P_SIZE)]


def packed_nodes(ref, v):
    return [packed_node(ref, v, i) for i in range(P_SIZE)]


def each_variable(work):
    def one(v, carry):
        work(v)
        return carry

    lax.fori_loop(0, V, one, 0, unroll=UNROLL)


def sublanes(x, shift):
    return pltpu.roll(x, shift % 8, 0) if shift % 8 else x


def pack_rows(pairs):
    _, row = iotas()
    out = []
    for p in range(3):
        block = pairs[2 * p]
        if 2 * p + 1 < P_SIZE:
            block = jnp.where(row % 2 == 0, block, sublanes(pairs[2 * p + 1], 1))
        out.append(block)
    return jnp.stack(out).reshape(24, TILE)


def packed_node(ref, v, i):
    return sublanes(block_of(ref, v, 24, (3, 8, TILE))[i // 2], -(i % 2))


def stage_mortar(nodes):
    _, row = iotas()
    spread = jnp.stack([jnp.stack([x, sublanes(x, -2)]) for x in nodes])
    return jnp.where(row % 4 == 0, spread, 0.0)


def surface_rows(values):
    _, row = iotas()
    return jnp.where(row % 4 < 2, values[0], sublanes(values[1], 2))


class Links:
    def __init__(self, send_sem, recv_sem):
        self.send_sem, self.recv_sem, self.started = send_sem, recv_sem, []

    def send(self, source, target, device):
        at = len(self.started)
        copy = pltpu.make_async_remote_copy(
            src_ref=source,
            dst_ref=target,
            send_sem=self.send_sem.at[at],
            recv_sem=self.recv_sem.at[at],
            device_id=device,
            device_id_type=MESH,
        )
        copy.start()
        self.started.append(copy)
        return copy

    def finish(self):
        for copy in self.started:
            copy.wait_send()


def neighbours(count, width, hops):
    me, block = lax.axis_index("azim"), lax.axis_index("rad")
    along = lambda o: {"azim": lax.rem(me + o % count, count)}
    beside = lambda o: {"rad": lax.rem(block + o % width, width)}
    hops = sorted({o % count for o in hops} - {0})
    sides = sorted({1 % width, -1 % width} - {0})
    barrier = pltpu.get_barrier_semaphore()
    for o in hops:
        pl.semaphore_signal(barrier, inc=1, device_id=along(-o), device_id_type=MESH)
    for o in sides:
        pl.semaphore_signal(barrier, inc=1, device_id=beside(-o), device_id_type=MESH)
    return along, beside, lambda: pl.semaphore_wait(barrier, len(hops) + len(sides))


def send_sides(links, bufs, along, beside):
    starts, finishes, lefts, rights, cols_out, cols_in = bufs
    return [
        links.send(starts, rights, along(-1)),
        links.send(finishes, lefts, along(1)),
        links.send(cols_out.at[0], cols_in.at[1], beside(-1)),
        links.send(cols_out.at[1], cols_in.at[0], beside(1)),
    ]


def columns_in(cols_in, width):
    block = lax.axis_index("rad")
    low = jnp.where(block > 0, cols_in[0], 0.0)
    high = jnp.where(block < width - 1, cols_in[1], 0.0)
    return low, high


def each_with_sides(work, starts, finishes, cols_out):
    def one(v, carry):
        x = work(v)
        put_edges(v, x, starts, finishes)
        return column_add(v, x, *carry)

    blank = jnp.zeros((8, TILE), jnp.float32)
    low, high = lax.fori_loop(0, V, one, (blank, blank), unroll=UNROLL)
    cols_out[0] = pltpu.roll(low, 4, 0)
    cols_out[1] = pltpu.roll(high, 4, 0)


def put_state(target, v, x):
    target[pl.ds(pl.multiple_of(v * 80, 80), 80), :] = x.reshape(80, TILE)


def surface_parts(field, starts, finishes, speeds, mixing, back, ends, begins):
    def work(v):
        x, rate = rates(v, field, None, None, None, None, speeds, mixing)
        values = x + (0.5 * time_step) * rate
        put_packed(back, v, [surface_rows(values[i]) for i in range(P_SIZE)])

    each_variable(work)
    for source, target in ((finishes, ends), (starts, begins)):
        layer = [surface_rows(block_of(source, v, 16, (2, 8, TILE))) for v in range(V)]
        target[...] = jnp.stack(layer).reshape(8 * V, TILE)


def opening(*refs):
    (
        field, rotor, speeds, mixing,
        first, second, starts, finishes, cols_out, back, ends, begins, own, wide,
    ) = refs
    own[...] = rotor[...].astype(jnp.float32)
    wide[...] = jnp.zeros_like(wide)
    for step, halves in enumerate((first, second)):
        each_variable(
            lambda v, step=step: put_packed(wide, v, [sublanes(x, -step) for x in nodes_of(own, v)])
        )
        halves[...] = wide[...].astype(jnp.bfloat16)
    each_with_sides(lambda v: state_of(field, v), starts, finishes, cols_out)
    surface_parts(field, starts, finishes, speeds, mixing, back, ends, begins)


def returned(v, back, ends, begins, low, high, speeds):
    lane, row = iotas()
    out = packed_nodes(back, v)
    scale = 0.5 * time_step
    out[0] = out[0] + (scale * P_SIZE) * speeds[v] * block_of(ends, v, 8, (8, TILE))
    out[-1] = out[-1] + (scale * penalty * P_SIZE) * block_of(begins, v, 8, (8, TILE))
    result = []
    for i, node in enumerate(out):
        spot = v * P_SIZE + i
        below = pltpu.roll(low, lax.rem(TILE - spot, TILE), 1)
        above = sublanes(pltpu.roll(high, TILE - 1 - spot, 1), 2)
        node = node + jnp.where((row == 0) & (lane == 0), scale * below, 0.0)
        result.append(node + jnp.where((row == 6) & (lane == TILE - 1), scale * above, 0.0))
    return result


def advance(step, count, width, *refs):
    (
        field, halves, far_own, far_prior, seam, lefts, rights, cols, back, ends, begins,
        back_cols, segment, *rest,
    ) = refs
    if step == 0:
        speeds, mixing, field_out, flux_out, *given = rest[:10]
        rest = rest[10:]
    else:
        flux, speeds, mixing, field_out, flux_out = rest[:5]
        rest = rest[5:]
    mid, mortar, weights, sides, own, prior, here, before, *bufs, send_sem, recv_sem = rest
    along, beside, entered = neighbours(count, width, (1, -1))
    for source, target in ((far_own, here), (far_prior, before), (halves, own), (seam, prior)):
        target[...] = source[...].astype(jnp.float32)
    mortar_tables(sublanes(segment[...], -step), weights, sides)

    def faced(v):
        nodes = mortar_nodes(packed_nodes(here, v), packed_nodes(before, v), weights, sides)
        put_packed(mortar, v, nodes)

    each_variable(faced)
    low, high = columns_in(cols, width)

    def first(v):
        x, rate = rates(v, field, lefts, rights, low, high, speeds, mixing)
        y = x + time_step * (rate + stage_mortar(packed_nodes(mortar, v)))
        put_state(mid, v, y)
        return y

    each_with_sides(first, bufs[0], bufs[1], bufs[4])
    entered()
    links = Links(send_sem, recv_sem)
    near = send_sides(links, bufs, along, beside)

    back_low, back_high = columns_in(back_cols, width)
    _, row = iotas()

    def flux_of(v):
        values = mortar_nodes(packed_nodes(own, v), packed_nodes(prior, v), weights, sides)
        seen = returned(v, back, ends, begins, back_low, back_high, speeds)
        out = [(1.0 - 0.5 * time_step) * a - b for a, b in zip(values, seen, strict=True)]
        if step == 0:
            put_packed(flux_out, v, out)
        else:
            pairs = zip(packed_nodes(flux, v), out, strict=True)
            both = [jnp.where(row % 2 == 0, a, sublanes(b, 1)) for a, b in pairs]
            at = pl.ds(pl.multiple_of(v * 40, 40), 40)
            flux_out[at, :] = jnp.stack(both).reshape(40, TILE)

    each_variable(flux_of)
    for copy in near:
        copy.wait_recv()
    mid_low, mid_high = columns_in(bufs[5], width)

    def second(v):
        y, rate = rates(v, mid, bufs[2], bufs[3], mid_low, mid_high, speeds, mixing)
        full = rate + stage_mortar(packed_nodes(mortar, v))
        new = 0.5 * (state_of(field, v) + y) + (0.5 * time_step) * full
        put_state(field_out, v, new)
        return new

    if step == 0:
        starts, finishes, cols_out, *parts = given
        each_with_sides(second, starts, finishes, cols_out)
        surface_parts(field_out, starts, finishes, speeds, mixing, *parts)
    else:
        each_variable(second)
    links.finish()


def exchange(shift, count, width, *refs):
    (
        halves, starts, finishes, cols, back, ends, begins,
        far_own, far_prior, seam, lefts, rights, cols_in, back_in, ends_in, begins_in,
        back_cols, send_sem, recv_sem,
    ) = refs
    me, block = lax.axis_index("azim"), lax.axis_index("rad")
    routes = [
        (halves, far_own, shift, 0),
        (back, back_in, -shift, 0),
        (halves, far_prior, shift + 1, 0),
        (ends, ends_in, 1 - shift, 0),
        (begins, begins_in, -1 - shift, 0),
        (cols.at[0], back_cols.at[1], -shift, -1),
        (cols.at[1], back_cols.at[0], -shift, 1),
        (starts, rights, -1, 0),
        (finishes, lefts, 1, 0),
        (halves, seam, 1, 0),
        (cols.at[0], cols_in.at[1], 0, -1),
        (cols.at[1], cols_in.at[0], 0, 1),
    ]
    copies = []
    for at, (source, target, o, d) in enumerate(routes):
        if o % count == 0 and d % width == 0:
            copy = pltpu.make_async_copy(source, target, recv_sem.at[at])
        else:
            device = {}
            if o % count:
                device["azim"] = lax.rem(me + o % count, count)
            if d % width:
                device["rad"] = lax.rem(block + d % width, width)
            copy = pltpu.make_async_remote_copy(
                src_ref=source,
                dst_ref=target,
                send_sem=send_sem.at[at],
                recv_sem=recv_sem.at[at],
                device_id=device,
                device_id_type=MESH,
            )
        copy.start()
        copies.append(copy)
    for copy in copies:
        copy.wait()


VMEM = pl.BlockSpec(memory_space=pltpu.VMEM)
ANY = pl.BlockSpec(memory_space=pl.ANY)
SMEM = pl.BlockSpec(memory_space=pltpu.SMEM)


def rows(*shape):
    return pltpu.VMEM((*shape, TILE), jnp.float32)


def side_buffers():
    return [rows(80) for _ in range(4)] + [rows(2, 8), rows(2, 8)]


def links_buffers(copies):
    return [pltpu.SemaphoreType.DMA((copies,)), pltpu.SemaphoreType.DMA((copies,))]


def shaped(*shape):
    return jax.ShapeDtypeStruct(shape, jnp.float32)


SIDES = ((80,), (80,), (2, 8), (120,), (40,), (40,))
ROUTES = 12


def half():
    return jax.ShapeDtypeStruct((TILE, TILE), jnp.bfloat16)


def call_opening(field, rotor, speeds, mixing):
    return pl.pallas_call(
        opening,
        out_shape=(half(), half(), *(shaped(*out, TILE) for out in SIDES)),
        in_specs=[VMEM, VMEM, SMEM, SMEM],
        out_specs=(VMEM,) * 8,
        scratch_shapes=[rows(200), rows(TILE)],
        compiler_params=pltpu.CompilerParams(vmem_limit_bytes=16 << 20),
    )(field, rotor, speeds, mixing)


def call_exchange(shift, count, width, *sources):
    outs = ((80,), (80,), (2, 8), (120,), (40,), (40,), (2, 8))
    return pl.pallas_call(
        functools.partial(exchange, shift, count, width),
        out_shape=(half(), half(), half(), *(shaped(*out, TILE) for out in outs)),
        in_specs=[ANY] * len(sources),
        out_specs=(ANY,) * 10,
        scratch_shapes=links_buffers(ROUTES),
        compiler_params=pltpu.CompilerParams(has_side_effects=True),
    )(*sources)


def call_advance(step, count, width, *operands):
    outs = ((400,), (120,), *SIDES) if step == 0 else ((400,), (200,))
    return pl.pallas_call(
        functools.partial(advance, step, count, width),
        out_shape=tuple(shaped(*out, TILE) for out in outs),
        in_specs=[VMEM] * (len(operands) - 2) + [SMEM, SMEM],
        out_specs=(VMEM,) * len(outs),
        scratch_shapes=[rows(400), rows(120), rows(200), rows(40)]
        + [rows(TILE)] * 4
        + side_buffers()
        + links_buffers(4),
        compiler_params=pltpu.CompilerParams(
            collective_id=step, has_side_effects=True, vmem_limit_bytes=16 << 20
        ),
    )(*operands)


def body(count, width, state, rotor_trace, speeds, mixing, offsets, segments):
    field = state.reshape(L, V, P_SIZE, 2, 2, TILE).transpose(1, 2, 4, 3, 0, 5)
    rotor = rotor_trace.reshape(STEPS, V, P_SIZE, 4, TILE).transpose(1, 2, 3, 0, 4)
    segment = segments.reshape(STEPS, 4, TILE).transpose(1, 0, 2)
    field, rotor, segment = (x.reshape(-1, TILE) for x in (field, rotor, segment))
    moves = [functools.partial(call_exchange, shift, count, width) for shift in range(count)]
    *halves, starts, finishes, cols, back, ends, begins = call_opening(field, rotor, speeds, mixing)
    sides = (starts, finishes, cols, back, ends, begins)
    flux = ()
    for step in range(STEPS):
        seen = lax.switch(offsets[step], moves, halves[step], *sides)
        field, flux, *sides = call_advance(
            step, count, width, field, halves[step], *seen, segment, *flux, speeds, mixing
        )
        flux = (flux,)
    new_state = field.reshape(V, P_SIZE, 2, 2, L, TILE).transpose(4, 0, 1, 3, 2, 5)
    rotor_flux = flux[0].reshape(V, P_SIZE, 4, STEPS, TILE).transpose(3, 0, 1, 2, 4)
    return new_state.reshape(state.shape), rotor_flux.reshape(rotor_trace.shape)


def solution(mesh):
    cells = P(None, None, None, "azim", "rad")
    return jax.shard_map(
        functools.partial(body, mesh.shape["azim"], mesh.shape["rad"]),
        mesh=mesh,
        in_specs=(cells, cells, P(), P(), P(), P(None, "rad")),
        out_specs=(cells, cells),
        check_vma=False,
    )
```

```python
import functools

import jax
import jax.numpy as jnp
import numpy as np
from jax import lax
from jax.experimental import pallas as pl
from jax.experimental.pallas import tpu as pltpu
from jax.sharding import PartitionSpec as P

P_SIZE = 5
STEPS = 2
SEG = 8
UNROLL = True
V = 5
L = 4
TILE = 128
MESH = pl.DeviceIdType.MESH
time_step = 0.05
penalty = 0.5


def basis_at(points, nodes):
    count = nodes.shape[0]
    values = np.ones((points.shape[0], count))
    for index in range(count):
        for other in range(count):
            if other != index:
                values[:, index] = (
                    values[:, index] * (points - nodes[other]) / (nodes[index] - nodes[other])
                )
    return values


def slope_at(points, nodes):
    count = nodes.shape[0]
    values = np.zeros((points.shape[0], count))
    for index in range(count):
        for skip in range(count):
            if skip == index:
                continue
            term = np.ones(points.shape[0]) / (nodes[index] - nodes[skip])
            for other in range(count):
                if other != index and other != skip:
                    term = term * (points - nodes[other]) / (nodes[index] - nodes[other])
            values[:, index] = values[:, index] + term
    return values


def build_tables():
    nodes = (np.arange(P_SIZE) + 0.5) / P_SIZE
    deriv = slope_at(nodes, nodes)
    edge_zero = basis_at(np.array([0.0]), nodes)[0]
    edge_one = basis_at(np.array([1.0]), nodes)[0]
    inside = np.zeros((SEG, P_SIZE), bool)
    table = np.zeros((SEG, P_SIZE, P_SIZE))
    for level in range(SEG):
        spots = 1.0 + nodes - level / SEG
        inside[level] = spots < 1.0
        table[level] = np.where(
            inside[level][:, None], basis_at(spots, nodes), basis_at(spots - 1.0, nodes)
        )
    as_floats = lambda a: np.asarray(a, np.float32).tolist()
    return as_floats(deriv), as_floats(edge_zero), as_floats(edge_one), as_floats(table), inside


DERIV, EDGE0, EDGE1, TABLE, INSIDE = build_tables()


def iotas():
    lane = lax.broadcasted_iota(jnp.int32, (8, TILE), 1)
    row = lax.broadcasted_iota(jnp.int32, (8, TILE), 0)
    return lane, row


def weighted(weights, parts):
    total = weights[0] * parts[0]
    for weight, part in zip(weights[1:], parts[1:], strict=True):
        total = total + weight * part
    return total


def edge_values(x):
    nodes = [x[k] for k in range(P_SIZE)]
    return weighted(EDGE0, nodes), weighted(EDGE1, nodes)


def column_add(v, x, low, high):
    lane, _ = iotas()
    for i in range(P_SIZE):
        spot = v * P_SIZE + i
        low = jnp.where(lane == spot, pltpu.roll(x[i, 0], spot, 1), low)
        high = jnp.where(lane == spot, pltpu.roll(x[i, 1], spot + 1, 1), high)
    return low, high


def put_edges(v, x, starts, finishes):
    start, finish = edge_values(x)
    at = pl.ds(pl.multiple_of(v * 16, 16), 16)
    starts[at, :] = start.reshape(16, TILE)
    finishes[at, :] = finish.reshape(16, TILE)


def block_of(ref, v, rows, shape):
    return ref[pl.ds(pl.multiple_of(v * rows, rows), rows), :].reshape(shape)


def state_of(ref, v):
    return block_of(ref, v, 80, (P_SIZE, 2, 8, TILE))


def rotor_of(ref, v):
    return block_of(ref, v, 40, (P_SIZE, 8, TILE))


def rates(v, field, lefts, rights, low, high, speeds, mixing):
    lane, row = iotas()
    x = state_of(field, v)
    start, finish = edge_values(x)
    left = block_of(lefts, v, 16, (2, 8, TILE))
    right = block_of(rights, v, 16, (2, 8, TILE))
    speed = speeds[v]
    nodes = [x[k] for k in range(P_SIZE)]
    out = []
    for i in range(P_SIZE):
        slope = weighted(DERIV[i], nodes)
        if i == 0:
            slope = slope + float(P_SIZE) * (start - left)
        out.append(-speed * slope)
    out[-1] = out[-1] + (penalty * P_SIZE) * (right - finish)
    result = jnp.stack(out)
    for w in range(V):
        result = result + mixing[v, w] * state_of(field, w)
    flat = x.reshape(10, 8, TILE)
    down = pltpu.roll(flat, 1, 2).reshape(x.shape)
    up = pltpu.roll(flat, TILE - 1, 2).reshape(x.shape)
    spots = [v * P_SIZE + i for i in range(P_SIZE)]
    low_in = jnp.stack([pltpu.roll(low, lax.rem(TILE - s, TILE), 1) for s in spots])
    high_in = jnp.stack([pltpu.roll(high, TILE - 1 - s, 1) for s in spots])
    wrapped_down = jnp.where(row < 4, low_in, pltpu.roll(down[:, 1], 4, 1))
    wrapped_up = jnp.where(row >= 4, high_in, pltpu.roll(up[:, 0], 4, 1))
    below = jnp.stack(
        [
            jnp.where(lane == 0, wrapped_down, down[:, 0]),
            jnp.where(lane == 0, down[:, 0], down[:, 1]),
        ],
        axis=1,
    )
    above = jnp.stack(
        [
            jnp.where(lane == TILE - 1, up[:, 1], up[:, 0]),
            jnp.where(lane == TILE - 1, wrapped_up, up[:, 1]),
        ],
        axis=1,
    )
    layer = row % 4
    inner = pltpu.roll(flat, 1, 1).reshape(x.shape)
    outer = pltpu.roll(flat, 7, 1).reshape(x.shape)
    inner = jnp.where(layer == 0, 0.0, inner)
    outer = jnp.where(layer == 3, 0.0, outer)
    return x, result + (below + above + inner + outer - 4.0 * x)


def put_packed(target, v, nodes):
    target[pl.ds(pl.multiple_of(v * 24, 24), 24), :] = pack_rows(nodes)


def mortar_tables(segment, weights, sides):
    for i in range(P_SIZE):
        side = jnp.zeros((8, TILE), jnp.float32)
        for level in range(1, SEG):
            if INSIDE[level, i]:
                side = jnp.where(segment == level, 1.0, side)
        sides[pl.ds(i * 8, 8), :] = side
        for k in range(P_SIZE):
            value = jnp.full((8, TILE), TABLE[1][i][k], jnp.float32)
            for level in range(2, SEG):
                value = jnp.where(segment == level, TABLE[level][i][k], value)
            weights[pl.ds((i * P_SIZE + k) * 8, 8), :] = value


def mortar_nodes(own, prior, weights, sides):
    out = []
    for i in range(P_SIZE):
        inside = sides[pl.ds(i * 8, 8), :] > 0.5
        picked = jnp.stack([jnp.where(inside, b, a) for a, b in zip(own, prior, strict=True)])
        factors = weights[pl.ds(i * 40, 40), :].reshape(P_SIZE, 8, TILE)
        out.append(jnp.sum(factors * picked, axis=0))
    return out


def nodes_of(ref, v):
    values = rotor_of(ref, v)
    return [values[i] for i in range(P_SIZE)]


def packed_nodes(ref, v):
    return [packed_node(ref, v, i) for i in range(P_SIZE)]


def each_variable(work):
    def one(v, carry):
        work(v)
        return carry

    lax.fori_loop(0, V, one, 0, unroll=UNROLL)


def sublanes(x, shift):
    return pltpu.roll(x, shift % 8, 0) if shift % 8 else x


def pack_rows(pairs):
    _, row = iotas()
    out = []
    for p in range(3):
        block = pairs[2 * p]
        if 2 * p + 1 < P_SIZE:
            block = jnp.where(row % 2 == 0, block, sublanes(pairs[2 * p + 1], 1))
        out.append(block)
    return jnp.stack(out).reshape(24, TILE)


def packed_node(ref, v, i):
    return sublanes(block_of(ref, v, 24, (3, 8, TILE))[i // 2], -(i % 2))


def stage_mortar(nodes):
    _, row = iotas()
    spread = jnp.stack([jnp.stack([x, sublanes(x, -2)]) for x in nodes])
    return jnp.where(row % 4 == 0, spread, 0.0)


def surface(x, rate):
    _, row = iotas()
    out = []
    for i in range(P_SIZE):
        both = x[i] + (0.5 * time_step) * rate[i]
        out.append(jnp.where(row % 4 < 2, both[0], sublanes(both[1], 2)))
    return out


class Links:
    def __init__(self, send_sem, recv_sem):
        self.send_sem, self.recv_sem, self.started = send_sem, recv_sem, []

    def send(self, source, target, device):
        at = len(self.started)
        copy = pltpu.make_async_remote_copy(
            src_ref=source,
            dst_ref=target,
            send_sem=self.send_sem.at[at],
            recv_sem=self.recv_sem.at[at],
            device_id=device,
            device_id_type=MESH,
        )
        copy.start()
        self.started.append(copy)
        return copy

    def finish(self):
        for copy in self.started:
            copy.wait_send()


def neighbours(count, width, hops):
    me, block = lax.axis_index("azim"), lax.axis_index("rad")
    along = lambda o: {"azim": lax.rem(me + o % count, count)}
    beside = lambda o: {"rad": lax.rem(block + o % width, width)}
    hops = sorted({o % count for o in hops} - {0})
    sides = sorted({1 % width, -1 % width} - {0})
    barrier = pltpu.get_barrier_semaphore()
    for o in hops:
        pl.semaphore_signal(barrier, inc=1, device_id=along(-o), device_id_type=MESH)
    for o in sides:
        pl.semaphore_signal(barrier, inc=1, device_id=beside(-o), device_id_type=MESH)
    return along, beside, lambda: pl.semaphore_wait(barrier, len(hops) + len(sides))


def send_sides(links, slot, bufs, along, beside):
    starts, finishes, lefts, rights, cols_out, cols_in = bufs
    return [
        links.send(starts.at[slot], rights.at[slot], along(-1)),
        links.send(finishes.at[slot], lefts.at[slot], along(1)),
        links.send(cols_out.at[slot, 0], cols_in.at[slot, 1], beside(-1)),
        links.send(cols_out.at[slot, 1], cols_in.at[slot, 0], beside(1)),
    ]


def columns_in(cols_in, slot, width):
    block = lax.axis_index("rad")
    low = jnp.where(block > 0, cols_in[slot, 0], 0.0)
    high = jnp.where(block < width - 1, cols_in[slot, 1], 0.0)
    return low, high


def put_columns(cols_out, slot, low, high):
    cols_out[slot, 0] = pltpu.roll(low, 4, 0)
    cols_out[slot, 1] = pltpu.roll(high, 4, 0)


def each_with_sides(work, slot, bufs):
    def one(v, carry):
        x = work(v)
        put_edges(v, x, bufs[0].at[slot], bufs[1].at[slot])
        return column_add(v, x, *carry)

    blank = jnp.zeros((8, TILE), jnp.float32)
    low, high = lax.fori_loop(0, V, one, (blank, blank), unroll=UNROLL)
    put_columns(bufs[4], slot, low, high)


def put_state(target, v, x):
    target[pl.ds(pl.multiple_of(v * 80, 80), 80), :] = x.reshape(80, TILE)


def begin(field, rate, mortar, mid, slot, bufs):
    def work(v):
        full = state_of(rate, v) + stage_mortar(packed_nodes(mortar, v))
        y = state_of(field, v) + time_step * full
        put_state(mid, v, y)
        return y

    each_with_sides(work, slot, bufs)


def conclude(field, mid, mortar, slot, bufs, speeds, mixing, width, target):
    low, high = columns_in(bufs[5], slot, width)

    def work(v):
        y, rate = rates(v, mid, bufs[2].at[slot], bufs[3].at[slot], low, high, speeds, mixing)
        full = rate + stage_mortar(packed_nodes(mortar, v))
        new = 0.5 * (state_of(field, v) + y) + (0.5 * time_step) * full
        put_state(target, v, new)
        return new

    return work


def look_ahead(field, slot, bufs, speeds, mixing, width, rate_out, back_out):
    low, high = columns_in(bufs[5], slot, width)

    def work(v):
        x, rate = rates(v, field, bufs[2].at[slot], bufs[3].at[slot], low, high, speeds, mixing)
        put_state(rate_out, v, rate)
        put_packed(back_out, v, surface(x, rate))

    each_variable(work)


def opening(count, width, *refs):
    (
        field, rotor, segment, speeds, mixing, rate_out, back_out, *outs,
    ) = refs[:9]
    (
        own, weights, sides, wide, halves, seam, *rest,
    ) = refs[9:]
    *bufs, send_sem, recv_sem = rest
    along, beside, entered = neighbours(count, width, (1, -1))
    own[...] = rotor[...].astype(jnp.float32)
    wide[...] = jnp.zeros_like(wide)
    for step in range(STEPS):
        each_variable(
            lambda v, step=step: put_packed(
                wide.at[step], v, [sublanes(x, -step) for x in nodes_of(own, v)]
            )
        )
    halves[...] = wide[...].astype(jnp.bfloat16)
    each_with_sides(lambda v: state_of(field, v), 0, bufs)

    entered()
    links = Links(send_sem, recv_sem)
    near = send_sides(links, 0, bufs, along, beside)
    seam_copy = links.send(halves, seam, along(1))
    mortar_tables(segment[...], weights, sides)
    for copy in near:
        copy.wait_recv()
    look_ahead(field, 0, bufs, speeds, mixing, width, rate_out, back_out)
    seam_copy.wait_recv()
    wide[...] = seam[...].astype(jnp.float32)
    for step in range(STEPS):

        def facing(v, step=step):
            before = [sublanes(x, step) for x in packed_nodes(wide.at[step], v)]
            values = mortar_nodes(nodes_of(own, v), before, weights, sides)
            put_packed(outs[step], v, [sublanes(x, -step) for x in values])

        each_variable(facing)
    links.finish()


def first_step(count, width, *refs):
    field, rate, mortar, speeds, mixing, field_out, rate_out, back_out, mid, *rest = refs
    *bufs, send_sem, recv_sem = rest
    along, beside, entered = neighbours(count, width, (1, -1))
    begin(field, rate, mortar, mid, 0, bufs)
    entered()
    links = Links(send_sem, recv_sem)
    for copy in send_sides(links, 0, bufs, along, beside):
        copy.wait_recv()
    work = conclude(field, mid, mortar, 0, bufs, speeds, mixing, width, field_out)
    each_with_sides(work, 1, bufs)
    for copy in send_sides(links, 1, bufs, along, beside):
        copy.wait_recv()
    look_ahead(field_out, 1, bufs, speeds, mixing, width, rate_out, back_out)
    links.finish()


def last_step(count, width, *refs):
    (
        field, rate, mortar, first, second, first_back, second_back, speeds, mixing,
        field_out, flux_out, mid, *rest,
    ) = refs
    *bufs, send_sem, recv_sem = rest
    along, beside, entered = neighbours(count, width, (1, -1))
    begin(field, rate, mortar, mid, 0, bufs)
    entered()
    links = Links(send_sem, recv_sem)
    near = send_sides(links, 0, bufs, along, beside)
    _, row = iotas()

    def flux(v):
        both = []
        for ready, back in ((first, first_back), (second, second_back)):
            own, seen = packed_nodes(ready, v), packed_nodes(back, v)
            both.append([(1.0 - 0.5 * time_step) * a - b for a, b in zip(own, seen, strict=True)])
        nodes = [jnp.where(row % 2 == 0, a, sublanes(b, 1)) for a, b in zip(*both, strict=True)]
        flux_out[pl.ds(pl.multiple_of(v * 40, 40), 40), :] = jnp.stack(nodes).reshape(40, TILE)

    each_variable(flux)
    for copy in near:
        copy.wait_recv()
    each_variable(conclude(field, mid, mortar, 0, bufs, speeds, mixing, width, field_out))
    links.finish()


def swap(shift, count, ready, back, mortar_out, back_out, send_sem, recv_sem):
    if shift % count == 0:
        kept = [
            pltpu.make_async_copy(source, target, recv_sem.at[at])
            for at, (source, target) in enumerate(((ready, mortar_out), (back, back_out)))
        ]
        for copy in kept:
            copy.start()
        for copy in kept:
            copy.wait()
        return
    me = lax.axis_index("azim")
    links = Links(send_sem, recv_sem)
    there, here = ({"azim": lax.rem(me + o % count, count)} for o in (shift, -shift))
    copies = [links.send(ready, mortar_out, there), links.send(back, back_out, here)]
    for copy in copies:
        copy.wait_recv()
    links.finish()


VMEM = pl.BlockSpec(memory_space=pltpu.VMEM)
ANY = pl.BlockSpec(memory_space=pl.ANY)
SMEM = pl.BlockSpec(memory_space=pltpu.SMEM)


def rows(*shape):
    return pltpu.VMEM((*shape, TILE), jnp.float32)


def side_buffers():
    return [rows(2, 80) for _ in range(4)] + [rows(2, 2, 8), rows(2, 2, 8)]


def links_buffers(copies):
    return [pltpu.SemaphoreType.DMA((copies,)), pltpu.SemaphoreType.DMA((copies,))]


def shaped(*shape):
    return jax.ShapeDtypeStruct(shape, jnp.float32)


def call(kernel, identity, outs, scratch, copies, *operands):
    slots = len(operands) - 2
    return pl.pallas_call(
        kernel,
        out_shape=tuple(shaped(*out, TILE) for out in outs),
        in_specs=[VMEM] * slots + [SMEM, SMEM],
        out_specs=(VMEM,) * len(outs),
        scratch_shapes=scratch + side_buffers() + links_buffers(copies),
        compiler_params=pltpu.CompilerParams(
            collective_id=identity, has_side_effects=True, vmem_limit_bytes=16 << 20
        ),
    )(*operands)


def call_swap(shift, count, ready, back):
    return pl.pallas_call(
        functools.partial(swap, shift, count),
        out_shape=(shaped(*ready.shape), shaped(*back.shape)),
        in_specs=[ANY, ANY],
        out_specs=(ANY, ANY),
        scratch_shapes=links_buffers(2),
        compiler_params=pltpu.CompilerParams(has_side_effects=True),
    )(ready, back)


def body(count, width, state, rotor_trace, speeds, mixing, offsets, segments):
    field = state.reshape(L, V, P_SIZE, 2, 2, TILE).transpose(1, 2, 4, 3, 0, 5)
    rotor = rotor_trace.reshape(STEPS, V, P_SIZE, 4, TILE).transpose(1, 2, 3, 0, 4)
    segment = segments.reshape(STEPS, 4, TILE).transpose(1, 0, 2)
    field, rotor, segment = (x.reshape(-1, TILE) for x in (field, rotor, segment))
    swaps = [functools.partial(call_swap, shift, count) for shift in range(count)]
    bind = lambda kernel: functools.partial(kernel, count, width)
    half = pltpu.VMEM((STEPS, TILE, TILE), jnp.bfloat16)

    rate, back, *ready = call(
        bind(opening), 0, ((400,), (120,), (120,), (120,)),
        [rows(200), rows(200), rows(40), rows(STEPS, TILE), half, half], 5,
        field, rotor, segment, speeds, mixing,
    )
    mortar, first_back = lax.switch(offsets[0], swaps, ready[0], back)
    field, rate, back = call(
        bind(first_step), 1, ((400,), (400,), (120,)), [rows(400)], 8,
        field, rate, mortar, speeds, mixing,
    )
    mortar, second_back = lax.switch(offsets[1], swaps, ready[1], back)
    field, flux = call(
        bind(last_step), 2, ((400,), (200,)), [rows(400)], 4,
        field, rate, mortar, *ready, first_back, second_back, speeds, mixing,
    )
    new_state = field.reshape(V, P_SIZE, 2, 2, L, TILE).transpose(4, 0, 1, 3, 2, 5)
    rotor_flux = flux.reshape(V, P_SIZE, 4, STEPS, TILE).transpose(3, 0, 1, 2, 4)
    return new_state.reshape(state.shape), rotor_flux.reshape(rotor_trace.shape)


def solution(mesh):
    cells = P(None, None, None, "azim", "rad")
    return jax.shard_map(
        functools.partial(body, mesh.shape["azim"], mesh.shape["rad"]),
        mesh=mesh,
        in_specs=(cells, cells, P(), P(), P(), P(None, "rad")),
        out_specs=(cells, cells),
        check_vma=False,
    )
```

```python
import functools

import jax
import jax.numpy as jnp
import numpy as np
from jax import lax
from jax.experimental import pallas as pl
from jax.experimental.pallas import tpu as pltpu
from jax.sharding import PartitionSpec as P

P_SIZE = 5
STEPS = 2
SEG = 8
UNROLL = True
V = 5
L = 4
TILE = 128
MESH = pl.DeviceIdType.MESH
time_step = 0.05
penalty = 0.5


def basis_at(points, nodes):
    count = nodes.shape[0]
    values = np.ones((points.shape[0], count))
    for index in range(count):
        for other in range(count):
            if other != index:
                values[:, index] = (
                    values[:, index] * (points - nodes[other]) / (nodes[index] - nodes[other])
                )
    return values


def slope_at(points, nodes):
    count = nodes.shape[0]
    values = np.zeros((points.shape[0], count))
    for index in range(count):
        for skip in range(count):
            if skip == index:
                continue
            term = np.ones(points.shape[0]) / (nodes[index] - nodes[skip])
            for other in range(count):
                if other != index and other != skip:
                    term = term * (points - nodes[other]) / (nodes[index] - nodes[other])
            values[:, index] = values[:, index] + term
    return values


def build_tables():
    nodes = (np.arange(P_SIZE) + 0.5) / P_SIZE
    deriv = slope_at(nodes, nodes)
    edge_zero = basis_at(np.array([0.0]), nodes)[0]
    edge_one = basis_at(np.array([1.0]), nodes)[0]
    inside = np.zeros((SEG, P_SIZE), bool)
    table = np.zeros((SEG, P_SIZE, P_SIZE))
    for level in range(SEG):
        spots = 1.0 + nodes - level / SEG
        inside[level] = spots < 1.0
        table[level] = np.where(
            inside[level][:, None], basis_at(spots, nodes), basis_at(spots - 1.0, nodes)
        )
    as_floats = lambda a: np.asarray(a, np.float32).tolist()
    return as_floats(deriv), as_floats(edge_zero), as_floats(edge_one), as_floats(table), inside


DERIV, EDGE0, EDGE1, TABLE, INSIDE = build_tables()


def iotas():
    lane = lax.broadcasted_iota(jnp.int32, (8, TILE), 1)
    row = lax.broadcasted_iota(jnp.int32, (8, TILE), 0)
    return lane, row


def weighted(weights, parts):
    total = weights[0] * parts[0]
    for weight, part in zip(weights[1:], parts[1:], strict=True):
        total = total + weight * part
    return total


def edge_values(x):
    nodes = [x[k] for k in range(P_SIZE)]
    return weighted(EDGE0, nodes), weighted(EDGE1, nodes)


def column_add(v, x, low, high):
    lane, _ = iotas()
    for i in range(P_SIZE):
        spot = v * P_SIZE + i
        low = jnp.where(lane == spot, pltpu.roll(x[i, 0], spot, 1), low)
        high = jnp.where(lane == spot, pltpu.roll(x[i, 1], spot + 1, 1), high)
    return low, high


def put_edges(v, x, starts, finishes):
    start, finish = edge_values(x)
    at = pl.ds(pl.multiple_of(v * 16, 16), 16)
    starts[at, :] = start.reshape(16, TILE)
    finishes[at, :] = finish.reshape(16, TILE)


def block_of(ref, v, rows, shape):
    return ref[pl.ds(pl.multiple_of(v * rows, rows), rows), :].reshape(shape)


def state_of(ref, v):
    return block_of(ref, v, 80, (P_SIZE, 2, 8, TILE))


def rotor_of(ref, v):
    return block_of(ref, v, 40, (P_SIZE, 8, TILE))


def rates(v, field, lefts, rights, low, high, speeds, mixing):
    lane, row = iotas()
    x = state_of(field, v)
    start, finish = edge_values(x)
    left = block_of(lefts, v, 16, (2, 8, TILE))
    right = block_of(rights, v, 16, (2, 8, TILE))
    speed = speeds[v]
    nodes = [x[k] for k in range(P_SIZE)]
    out = []
    for i in range(P_SIZE):
        slope = weighted(DERIV[i], nodes)
        if i == 0:
            slope = slope + float(P_SIZE) * (start - left)
        out.append(-speed * slope)
    out[-1] = out[-1] + (penalty * P_SIZE) * (right - finish)
    result = jnp.stack(out)
    for w in range(V):
        result = result + mixing[v, w] * state_of(field, w)
    flat = x.reshape(10, 8, TILE)
    down = pltpu.roll(flat, 1, 2).reshape(x.shape)
    up = pltpu.roll(flat, TILE - 1, 2).reshape(x.shape)
    spots = [v * P_SIZE + i for i in range(P_SIZE)]
    low_in = jnp.stack([pltpu.roll(low, lax.rem(TILE - s, TILE), 1) for s in spots])
    high_in = jnp.stack([pltpu.roll(high, TILE - 1 - s, 1) for s in spots])
    wrapped_down = jnp.where(row < 4, low_in, pltpu.roll(down[:, 1], 4, 1))
    wrapped_up = jnp.where(row >= 4, high_in, pltpu.roll(up[:, 0], 4, 1))
    below = jnp.stack(
        [
            jnp.where(lane == 0, wrapped_down, down[:, 0]),
            jnp.where(lane == 0, down[:, 0], down[:, 1]),
        ],
        axis=1,
    )
    above = jnp.stack(
        [
            jnp.where(lane == TILE - 1, up[:, 1], up[:, 0]),
            jnp.where(lane == TILE - 1, wrapped_up, up[:, 1]),
        ],
        axis=1,
    )
    layer = row % 4
    inner = pltpu.roll(flat, 1, 1).reshape(x.shape)
    outer = pltpu.roll(flat, 7, 1).reshape(x.shape)
    inner = jnp.where(layer == 0, 0.0, inner)
    outer = jnp.where(layer == 3, 0.0, outer)
    return x, result + (below + above + inner + outer - 4.0 * x)


def put_packed(target, v, nodes):
    _, row = iotas()
    pairs = [
        jnp.where(row % 2 == 0, nodes[at], sublanes(nodes[at + 1], 1)) for at in range(0, P_SIZE - 1, 2)
    ]
    target[pl.ds(pl.multiple_of(v * 16, 16), 16), :] = jnp.stack(pairs).reshape(16, TILE)
    at = pl.ds(pl.multiple_of(16 * V + v // 2 * 8, 8), 8)
    odd = jnp.where(row % 2 == 0, target[at, :], sublanes(nodes[-1], 1))
    target[at, :] = jnp.where(v % 2 == 0, nodes[-1], odd)


def mortar_tables(segment, weights, sides):
    for i in range(P_SIZE):
        side = jnp.zeros((8, TILE), jnp.float32)
        for level in range(1, SEG):
            if INSIDE[level, i]:
                side = jnp.where(segment == level, 1.0, side)
        sides[pl.ds(i * 8, 8), :] = side
        for k in range(P_SIZE):
            value = jnp.full((8, TILE), TABLE[1][i][k], jnp.float32)
            for level in range(2, SEG):
                value = jnp.where(segment == level, TABLE[level][i][k], value)
            weights[pl.ds((i * P_SIZE + k) * 8, 8), :] = value


def mortar_nodes(own, prior, weights, sides):
    out = []
    for i in range(P_SIZE):
        inside = sides[pl.ds(i * 8, 8), :] > 0.5
        picked = jnp.stack([jnp.where(inside, b, a) for a, b in zip(own, prior, strict=True)])
        factors = weights[pl.ds(i * 40, 40), :].reshape(P_SIZE, 8, TILE)
        out.append(jnp.sum(factors * picked, axis=0))
    return out


def nodes_of(ref, v):
    values = rotor_of(ref, v)
    return [values[i] for i in range(P_SIZE)]


def each_variable(work):
    def one(v, carry):
        work(v)
        return carry

    lax.fori_loop(0, V, one, 0, unroll=UNROLL)


def sublanes(x, shift):
    return pltpu.roll(x, shift % 8, 0) if shift % 8 else x


def packed_nodes(ref, v):
    pairs = block_of(ref, v, 16, (2, 8, TILE))
    out = [sublanes(pairs[i // 2], -(i % 2)) for i in range(P_SIZE - 1)]
    last = ref[pl.ds(pl.multiple_of(16 * V + v // 2 * 8, 8), 8), :]
    return [*out, jnp.where(v % 2 == 0, last, sublanes(last, -1))]


def stage_mortar(nodes):
    _, row = iotas()
    spread = jnp.stack([jnp.stack([x, sublanes(x, -2)]) for x in nodes])
    return jnp.where(row % 4 == 0, spread, 0.0)


def surface(x, rate):
    _, row = iotas()
    out = []
    for i in range(P_SIZE):
        both = x[i] + (0.5 * time_step) * rate[i]
        out.append(jnp.where(row % 4 < 2, both[0], sublanes(both[1], 2)))
    return out


class Links:
    def __init__(self, send_sem, recv_sem):
        self.send_sem, self.recv_sem, self.started = send_sem, recv_sem, []

    def send(self, source, target, device):
        at = len(self.started)
        copy = pltpu.make_async_remote_copy(
            src_ref=source,
            dst_ref=target,
            send_sem=self.send_sem.at[at],
            recv_sem=self.recv_sem.at[at],
            device_id=device,
            device_id_type=MESH,
        )
        copy.start()
        self.started.append(copy)
        return copy

    def finish(self):
        for copy in self.started:
            copy.wait_send()


def neighbours(count, width, hops):
    me, block = lax.axis_index("azim"), lax.axis_index("rad")
    along = lambda o: {"azim": lax.rem(me + o % count, count)}
    beside = lambda o: {"rad": lax.rem(block + o % width, width)}
    hops = sorted({o % count for o in hops} - {0})
    sides = sorted({1 % width, -1 % width} - {0})
    barrier = pltpu.get_barrier_semaphore()
    for o in hops:
        pl.semaphore_signal(barrier, inc=1, device_id=along(-o), device_id_type=MESH)
    for o in sides:
        pl.semaphore_signal(barrier, inc=1, device_id=beside(-o), device_id_type=MESH)
    return along, beside, lambda: pl.semaphore_wait(barrier, len(hops) + len(sides))


def send_sides(links, slot, bufs, along, beside):
    starts, finishes, lefts, rights, cols_out, cols_in = bufs
    return [
        links.send(starts.at[slot], rights.at[slot], along(-1)),
        links.send(finishes.at[slot], lefts.at[slot], along(1)),
        links.send(cols_out.at[slot, 0], cols_in.at[slot, 1], beside(-1)),
        links.send(cols_out.at[slot, 1], cols_in.at[slot, 0], beside(1)),
    ]


def columns_in(cols_in, slot, width):
    block = lax.axis_index("rad")
    low = jnp.where(block > 0, cols_in[slot, 0], 0.0)
    high = jnp.where(block < width - 1, cols_in[slot, 1], 0.0)
    return low, high


def put_columns(cols_out, slot, low, high):
    cols_out[slot, 0] = pltpu.roll(low, 4, 0)
    cols_out[slot, 1] = pltpu.roll(high, 4, 0)


def each_with_sides(work, slot, bufs):
    def one(v, carry):
        x = work(v)
        put_edges(v, x, bufs[0].at[slot], bufs[1].at[slot])
        return column_add(v, x, *carry)

    blank = jnp.zeros((8, TILE), jnp.float32)
    low, high = lax.fori_loop(0, V, one, (blank, blank), unroll=UNROLL)
    put_columns(bufs[4], slot, low, high)


def put_state(target, v, x):
    target[pl.ds(pl.multiple_of(v * 80, 80), 80), :] = x.reshape(80, TILE)


def begin(field, rate, mortar, mid, slot, bufs):
    def work(v):
        full = state_of(rate, v) + stage_mortar(packed_nodes(mortar, v))
        y = state_of(field, v) + time_step * full
        put_state(mid, v, y)
        return y

    each_with_sides(work, slot, bufs)


def conclude(field, mid, mortar, slot, bufs, speeds, mixing, width, target):
    low, high = columns_in(bufs[5], slot, width)

    def work(v):
        y, rate = rates(v, mid, bufs[2].at[slot], bufs[3].at[slot], low, high, speeds, mixing)
        full = rate + stage_mortar(packed_nodes(mortar, v))
        new = 0.5 * (state_of(field, v) + y) + (0.5 * time_step) * full
        put_state(target, v, new)
        return new

    return work


def look_ahead(field, slot, bufs, speeds, mixing, width, rate_out, back_out):
    low, high = columns_in(bufs[5], slot, width)

    def work(v):
        x, rate = rates(v, field, bufs[2].at[slot], bufs[3].at[slot], low, high, speeds, mixing)
        put_state(rate_out, v, rate)
        put_packed(back_out, v, surface(x, rate))

    each_variable(work)


def opening(count, width, *refs):
    (
        field, rotor, segment, speeds, mixing, rate_out, back_out, *outs,
    ) = refs[:9]
    (
        own, weights, sides, wide, halves, seam, *rest,
    ) = refs[9:]
    *bufs, send_sem, recv_sem = rest
    along, beside, entered = neighbours(count, width, (1, -1))
    own[...] = rotor[...].astype(jnp.float32)
    wide[...] = jnp.zeros_like(wide)
    for step in range(STEPS):
        each_variable(
            lambda v, step=step: put_packed(
                wide.at[step], v, [sublanes(x, -step) for x in nodes_of(own, v)]
            )
        )
    halves[...] = wide[...].astype(jnp.bfloat16)
    each_with_sides(lambda v: state_of(field, v), 0, bufs)

    entered()
    links = Links(send_sem, recv_sem)
    near = send_sides(links, 0, bufs, along, beside)
    seam_copy = links.send(halves, seam, along(1))
    mortar_tables(segment[...], weights, sides)
    for copy in near:
        copy.wait_recv()
    look_ahead(field, 0, bufs, speeds, mixing, width, rate_out, back_out)
    seam_copy.wait_recv()
    wide[...] = seam[...].astype(jnp.float32)
    for step in range(STEPS):

        def facing(v, step=step):
            before = [sublanes(x, step) for x in packed_nodes(wide.at[step], v)]
            values = mortar_nodes(nodes_of(own, v), before, weights, sides)
            put_packed(outs[step], v, [sublanes(x, -step) for x in values])

        each_variable(facing)
    links.finish()


def first_step(count, width, *refs):
    field, rate, mortar, speeds, mixing, field_out, rate_out, back_out, mid, *rest = refs
    *bufs, send_sem, recv_sem = rest
    along, beside, entered = neighbours(count, width, (1, -1))
    begin(field, rate, mortar, mid, 0, bufs)
    entered()
    links = Links(send_sem, recv_sem)
    for copy in send_sides(links, 0, bufs, along, beside):
        copy.wait_recv()
    work = conclude(field, mid, mortar, 0, bufs, speeds, mixing, width, field_out)
    each_with_sides(work, 1, bufs)
    for copy in send_sides(links, 1, bufs, along, beside):
        copy.wait_recv()
    look_ahead(field_out, 1, bufs, speeds, mixing, width, rate_out, back_out)
    links.finish()


def last_step(count, width, *refs):
    (
        field, rate, mortar, first, second, first_back, second_back, speeds, mixing,
        field_out, flux_out, mid, *rest,
    ) = refs
    *bufs, send_sem, recv_sem = rest
    along, beside, entered = neighbours(count, width, (1, -1))
    begin(field, rate, mortar, mid, 0, bufs)
    entered()
    links = Links(send_sem, recv_sem)
    near = send_sides(links, 0, bufs, along, beside)
    _, row = iotas()

    def flux(v):
        both = []
        for ready, back in ((first, first_back), (second, second_back)):
            own, seen = packed_nodes(ready, v), packed_nodes(back, v)
            both.append([(1.0 - 0.5 * time_step) * a - b for a, b in zip(own, seen, strict=True)])
        nodes = [jnp.where(row % 2 == 0, a, sublanes(b, 1)) for a, b in zip(*both, strict=True)]
        flux_out[pl.ds(pl.multiple_of(v * 40, 40), 40), :] = jnp.stack(nodes).reshape(40, TILE)

    each_variable(flux)
    for copy in near:
        copy.wait_recv()
    each_variable(conclude(field, mid, mortar, 0, bufs, speeds, mixing, width, field_out))
    links.finish()


def swap(shift, count, ready, back, mortar_out, back_out, send_sem, recv_sem):
    if shift % count == 0:
        kept = [
            pltpu.make_async_copy(source, target, recv_sem.at[at])
            for at, (source, target) in enumerate(((ready, mortar_out), (back, back_out)))
        ]
        for copy in kept:
            copy.start()
        for copy in kept:
            copy.wait()
        return
    me = lax.axis_index("azim")
    links = Links(send_sem, recv_sem)
    there, here = ({"azim": lax.rem(me + o % count, count)} for o in (shift, -shift))
    copies = [links.send(ready, mortar_out, there), links.send(back, back_out, here)]
    for copy in copies:
        copy.wait_recv()
    links.finish()


VMEM = pl.BlockSpec(memory_space=pltpu.VMEM)
ANY = pl.BlockSpec(memory_space=pl.ANY)
SMEM = pl.BlockSpec(memory_space=pltpu.SMEM)


def rows(*shape):
    return pltpu.VMEM((*shape, TILE), jnp.float32)


def side_buffers():
    return [rows(2, 80) for _ in range(4)] + [rows(2, 2, 8), rows(2, 2, 8)]


def links_buffers(copies):
    return [pltpu.SemaphoreType.DMA((copies,)), pltpu.SemaphoreType.DMA((copies,))]


def shaped(*shape):
    return jax.ShapeDtypeStruct(shape, jnp.float32)


def call(kernel, identity, outs, scratch, copies, *operands):
    slots = len(operands) - 2
    return pl.pallas_call(
        kernel,
        out_shape=tuple(shaped(*out, TILE) for out in outs),
        in_specs=[VMEM] * slots + [SMEM, SMEM],
        out_specs=(VMEM,) * len(outs),
        scratch_shapes=scratch + side_buffers() + links_buffers(copies),
        compiler_params=pltpu.CompilerParams(
            collective_id=identity, has_side_effects=True, vmem_limit_bytes=16 << 20
        ),
    )(*operands)


def call_swap(shift, count, ready, back):
    return pl.pallas_call(
        functools.partial(swap, shift, count),
        out_shape=(shaped(*ready.shape), shaped(*back.shape)),
        in_specs=[ANY, ANY],
        out_specs=(ANY, ANY),
        scratch_shapes=links_buffers(2),
        compiler_params=pltpu.CompilerParams(has_side_effects=True),
    )(ready, back)


def body(count, width, state, rotor_trace, speeds, mixing, offsets, segments):
    field = state.reshape(L, V, P_SIZE, 2, 2, TILE).transpose(1, 2, 4, 3, 0, 5)
    rotor = rotor_trace.reshape(STEPS, V, P_SIZE, 4, TILE).transpose(1, 2, 3, 0, 4)
    segment = segments.reshape(STEPS, 4, TILE).transpose(1, 0, 2)
    field, rotor, segment = (x.reshape(-1, TILE) for x in (field, rotor, segment))
    swaps = [functools.partial(call_swap, shift, count) for shift in range(count)]
    bind = lambda kernel: functools.partial(kernel, count, width)
    half = pltpu.VMEM((STEPS, TILE, TILE), jnp.bfloat16)

    rate, back, *ready = call(
        bind(opening), 0, ((400,), (104,), (104,), (104,)),
        [rows(200), rows(200), rows(40), rows(STEPS, TILE), half, half], 5,
        field, rotor, segment, speeds, mixing,
    )
    mortar, first_back = lax.switch(offsets[0], swaps, ready[0], back)
    field, rate, back = call(
        bind(first_step), 1, ((400,), (400,), (104,)), [rows(400)], 8,
        field, rate, mortar, speeds, mixing,
    )
    mortar, second_back = lax.switch(offsets[1], swaps, ready[1], back)
    field, flux = call(
        bind(last_step), 2, ((400,), (200,)), [rows(400)], 4,
        field, rate, mortar, *ready, first_back, second_back, speeds, mixing,
    )
    new_state = field.reshape(V, P_SIZE, 2, 2, L, TILE).transpose(4, 0, 1, 3, 2, 5)
    rotor_flux = flux.reshape(V, P_SIZE, 4, STEPS, TILE).transpose(3, 0, 1, 2, 4)
    return new_state.reshape(state.shape), rotor_flux.reshape(rotor_trace.shape)


def solution(mesh):
    cells = P(None, None, None, "azim", "rad")
    return jax.shard_map(
        functools.partial(body, mesh.shape["azim"], mesh.shape["rad"]),
        mesh=mesh,
        in_specs=(cells, cells, P(), P(), P(), P(None, "rad")),
        out_specs=(cells, cells),
        check_vma=False,
    )
```
